32 devices in a mesh: ctx: 16 (over z, y, x), dp: 2 (over core).
Axes of the slice: x: 2, y: 2, z: 4, core: 2. Of those that a mesh axis runs over, the one named last changes fastest.
Arguments:
- layer_input: bfloat16 [4, 1024, 4096], P('dp', 'ctx'), may hold values from -0.5 to 0.5
- queries: bfloat16 [4, 1024, 1024], P('dp', 'ctx'), may hold values from -8 to 8
- key_states: bfloat16 [4, 1024, 128], P('dp', 'ctx'), may hold values from -8 to 8
- value_states: bfloat16 [4, 1024, 128], P('dp', 'ctx'), may hold values from -6 to 6
- attn_output: bfloat16 [4, 1024, 1024], P('dp', 'ctx'), may hold values from -6 to 6
- out_grad: bfloat16 [4, 1024, 1024], P('dp', 'ctx'), may hold values from -6 to 6
- doc_ids: int32 [4, 1024], P('dp'), may hold values from 0 to 7, never falling along the last dimension, each value on 1 to 256 neighbouring positions
- positions: int32 [4, 1024], P('dp'), may hold values from 0 to 1023, as said below
Outputs:
- query_grad: bfloat16 [4, 1024, 1024], P('dp', 'ctx')
- kv_weight_grad: float32 [4096, 256], P('ctx')
The draws below stay inside these ranges and needn't reach their ends.
Inputs may be any that keep to these rules, and one draw needn't show every extreme that they name: `positions`: stored row c * 64 + r of a sequence (c below 16, r below 64) holds a position from r * (16) to (r + 1) * 16 - 1; every position of a sequence is held by exactly one row.
All inputs are finite; a program needn't handle non-finite values.
Results may differ from the reference program's by a relative error of at most 0.005.
Values may be sent and summed in bfloat16 or wider, within the bound.
A program may use at most 64 MiB of HBM per device.

```python
import math
import jax
import jax.numpy as jnp
import numpy as np
from jax import lax

D = 4096
HEADS = 8
HD = 128
SROWS = 64
SEQ_LEN = 1024
BATCH = 4
DOCS = 8
DOC_MOST = 256


def draw_queries(key, part):
    first_key = jax.random.fold_in(key, 0)
    whole_shape = (BATCH, SEQ_LEN, HEADS * HD)
    return jax.random.truncated_normal(first_key, -4.0, 4.0, whole_shape, jnp.float32).astype(jnp.bfloat16)


def draw_key_states(key, part):
    first_key = jax.random.fold_in(jax.random.fold_in(key, 7), 0)
    whole_shape = (BATCH, SEQ_LEN, HD)
    return jax.random.truncated_normal(first_key, -4.0, 4.0, whole_shape, jnp.float32).astype(jnp.bfloat16)


def draw_positions(key, part):
    device_count = SEQ_LEN // SROWS
    round_keys = jax.random.split(jax.random.fold_in(key, 11), BATCH * SROWS)
    orders = jax.vmap(lambda round_key: jax.random.permutation(round_key, device_count))(round_keys)
    orders = orders.reshape(BATCH, SROWS, device_count).astype(jnp.int32)
    round_base = (jnp.arange(SROWS, dtype=jnp.int32) * device_count)[None, :, None]
    placed = round_base + orders
    return placed.transpose(0, 2, 1).reshape(BATCH, SEQ_LEN)


def spiked(drawn, stream_key, source, target, blocks, factor):
    owner, partner = [(jnp.arange(drawn.shape[axis_at]) // (drawn.shape[axis_at] // blocks)).reshape([-1 if axis == axis_at else 1 for axis in range(drawn.ndim)]) for axis_at in (source, target)]
    chosen = jax.random.permutation(stream_key, blocks)[partner]
    strong = (owner == chosen) | (owner == (partner + blocks // 2) % blocks)
    return jnp.where(strong, factor * drawn, drawn)


def level_of(key, extent, pieces, low, high):
    level, own = 1.0, jax.random.fold_in(key, 6)
    for axis_at, shards_of in pieces:
        draws = jnp.exp(jax.random.uniform(jax.random.fold_in(own, axis_at), (shards_of,), jnp.float32, low / len(pieces), high / len(pieces)))
        level = level * jnp.repeat(draws, extent[axis_at] // shards_of).reshape([-1 if axis == axis_at else 1 for axis in range(len(extent))])
    return level


def profile(count, total, reach, lean):
    weights = [(1 << 20) // math.isqrt(rank ** lean) + 1 for rank in range(2, count + 1)]
    surplus, counts = total - reach - (count - 1), [1] * (count - 1)
    while surplus > 0:
        free = [i for i in range(count - 1) if counts[i] < reach]
        mass, left = sum([weights[i] for i in free]), surplus
        for i in free:
            extra = min(reach - counts[i], max(1, left * weights[i] // mass), surplus)
            counts[i] = counts[i] + extra
            surplus = surplus - extra
    return np.array([reach] + counts)


def ragged_sizes(stream_key, number_of, total, limit, slope):
    if number_of == 2:
        one = jax.random.randint(stream_key, (), max(1, total - limit), min(limit, total - 1) + 1)
        return jnp.stack([one, total - one])
    sizes = jnp.asarray(profile(number_of, total, limit, slope), jnp.int32)
    twos = (number_of - 1) // 2
    donor, taker = sizes[1:1 + 2 * twos:2], sizes[2:2 + 2 * twos:2]
    room = jnp.minimum(donor - 1, limit - taker)
    shifted = jax.random.randint(jax.random.fold_in(stream_key, 1), (twos,), 0, 1 << 20) % (room + 1)
    sizes = sizes.at[1:1 + 2 * twos:2].set(donor - shifted).at[2:2 + 2 * twos:2].set(taker + shifted)
    return sizes[jax.random.permutation(jax.random.fold_in(stream_key, 2), number_of)]


def centred(key, shape, spread, bound, pieces=(), kind=jnp.bfloat16):
    level = level_of(key, shape, pieces, -0.22, 0.18) if pieces else 1.0
    drawn = jax.random.normal(key, shape, jnp.float32) * spread * level
    return jnp.minimum(jnp.maximum(drawn, -bound), bound).astype(kind)


def heavy_noise(rng, extent, deviation, most, cuts, heavy, held_as=jnp.bfloat16):
    values = deviation * jax.random.normal(rng, extent, jnp.float32)
    if cuts:
        values = values * level_of(rng, extent, cuts, -0.22, 0.18)
    return jnp.clip(spiked(values, jax.random.fold_in(rng, 3), *heavy), -most, most).astype(held_as)


def setup_inputs(seed: int = 0) -> dict:
    key_list = jax.random.split(jax.random.key(seed), 9)
    layer_input = heavy_noise(key_list[0], (BATCH, SEQ_LEN, D), 0.0625, 0.5, ((0, 2), (1, 16)), (1, 2, 16, 2.0))
    queries = draw_queries(jax.random.fold_in(key_list[8], 71), 0)
    key_states = draw_key_states(jax.random.fold_in(key_list[8], 71), 0)
    value_states = centred(key_list[3], (BATCH, SEQ_LEN, HD), 1.0, 6.0, ((0, 2), (1, 16)))
    attn_output = centred(key_list[4], (BATCH, SEQ_LEN, HEADS * HD), 1.0, 6.0, ((0, 2), (1, 16)))
    out_grad = centred(key_list[5], (BATCH, SEQ_LEN, HEADS * HD), 1.0, 6.0, ((0, 2), (1, 16)))
    doc_ids = jax.vmap(lambda own: jnp.searchsorted(jnp.cumsum(ragged_sizes(own, DOCS, SEQ_LEN, DOC_MOST, 2)), jnp.arange(SEQ_LEN), side="right"))(jax.random.split(key_list[6], BATCH)).reshape((BATCH, SEQ_LEN)).astype(jnp.int32)
    positions = draw_positions(jax.random.fold_in(key_list[8], 71), 0)
    return dict(layer_input=layer_input, queries=queries, key_states=key_states, value_states=value_states, attn_output=attn_output, out_grad=out_grad, doc_ids=doc_ids, positions=positions)


NEG_FILL = -1e+30

def one_sequence(operands):
    query_seq, key_seq, value_seq, output_seq, grad_seq, doc_seq, pos_seq = operands
    seq_length = key_seq.shape[0]
    head_size = key_seq.shape[1]
    head_count = query_seq.shape[1] // head_size
    score_scale = 1.0 / math.sqrt(head_size)
    doc_rows = jnp.take(doc_seq, pos_seq)
    live_pairs = (doc_rows[:, None] == doc_rows[None, :]) & (pos_seq[None, :] <= pos_seq[:, None])
    query_heads = query_seq.reshape(seq_length, head_count, head_size).transpose(1, 0, 2)
    output_heads = output_seq.reshape(seq_length, head_count, head_size).transpose(1, 0, 2)
    grad_heads = grad_seq.reshape(seq_length, head_count, head_size).transpose(1, 0, 2)

    def one_head(key_accum, head_operands):
        query_head, output_head, grad_head = head_operands
        scores = jnp.dot(query_head, key_seq.T, preferred_element_type=jnp.float32) * score_scale
        masked = jnp.where(live_pairs, scores, NEG_FILL)
        row_max = lax.optimization_barrier(jnp.max(masked, axis=1))
        row_sum = lax.optimization_barrier(jnp.sum(jnp.where(live_pairs, jnp.exp(scores - row_max[:, None]), 0.0), axis=1))
        log_total = row_max + jnp.log(row_sum)
        probs = jnp.where(live_pairs, jnp.exp(scores - log_total[:, None]), 0.0)
        probs_half = probs.astype(jnp.bfloat16)
        row_delta = lax.optimization_barrier(jnp.sum(grad_head.astype(jnp.float32) * output_head.astype(jnp.float32), axis=1))
        prob_grad = jnp.dot(grad_head, value_seq.T, preferred_element_type=jnp.float32)
        score_grad = (probs * (prob_grad - row_delta[:, None])).astype(jnp.bfloat16)
        query_grad = (jnp.dot(score_grad, key_seq, preferred_element_type=jnp.float32) * score_scale).astype(jnp.bfloat16)
        key_grad = jnp.dot(score_grad.T, query_head, preferred_element_type=jnp.float32) * score_scale
        value_grad = jnp.dot(probs_half.T, grad_head, preferred_element_type=jnp.float32)
        return (key_accum + jnp.concatenate([key_grad, value_grad], axis=1), query_grad)
    start_accum = jnp.zeros((seq_length, 2 * head_size), jnp.float32)
    key_total, query_parts = lax.scan(one_head, start_accum, (query_heads, output_heads, grad_heads))
    query_rows = query_parts.transpose(1, 0, 2).reshape(seq_length, head_count * head_size)
    return (query_rows, key_total)

def reference(layer_input, queries, key_states, value_states, attn_output, out_grad, doc_ids, positions):
    query_grad, key_totals = lax.map(one_sequence, (queries, key_states, value_states, attn_output, out_grad, doc_ids, positions))
    kv_grad = key_totals.astype(jnp.bfloat16)
    model_width = layer_input.shape[2]
    flat_input = layer_input.reshape(-1, model_width)
    flat_grad = kv_grad.reshape(-1, kv_grad.shape[2])
    kv_weight_grad = lax.dot_general(flat_input, flat_grad, (((0,), (0,)), ((), ())), preferred_element_type=jnp.float32)
    return (query_grad, kv_weight_grad)
```

```python
import functools
import math

import jax
import jax.numpy as jnp
from jax import lax
from jax.experimental import pallas as pl
from jax.experimental.pallas import tpu as pltpu
from jax.sharding import PartitionSpec as P

NEG_FILL = -1e30
INNER = 4
LANES = 128


def kernel(
    dims,
    x_ref,
    q_ref,
    k_ref,
    v_ref,
    a_ref,
    g_ref,
    doc_ref,
    pos_ref,
    dq_ref,
    dw_ref,
    kv,
    kpos,
    dcol,
    acc,
    plane_out,
    plane_in,
    plane_sum,
    outer_out,
    outer_in,
    kvg,
    xg,
    wsum,
    w_out,
    w_in,
    w_fin,
    ag_send,
    ag_recv,
    plane_send,
    plane_recv,
    outer_send,
    outer_recv,
    kvg_send,
    kvg_recv,
    x_send,
    x_recv,
    w_send,
    w_recv,
    fin_send,
    fin_recv,
    own_sem,
):
    outer, pairs, width = dims
    seqs, rows, head = k_ref.shape
    heads = q_ref.shape[2] // head
    groups = 4
    step = rows // groups
    lanes_n = heads * step
    scale = 1.0 / math.sqrt(head)
    x_parts = xg.shape[1] if x_ref.ndim == 2 else 1

    me = lax.axis_index("ctx")
    pair = lax.axis_index("dp")
    o_me, i_me = me // INNER, me % INNER

    def inner_of(k):
        low = (i_me % 2 + k % 2) % 2
        high = (i_me // 2 + k // 2) % 2
        return high * 2 + low

    def outer_of(m):
        return (o_me + m) % outer

    def ctx_of(o, i):
        return o * INNER + i

    def copy_to(src, dst, send_sem, recv_sem, ctx, dp):
        return pltpu.make_async_remote_copy(
            src_ref=src,
            dst_ref=dst,
            send_sem=send_sem,
            recv_sem=recv_sem,
            device_id={"ctx": ctx, "dp": dp},
            device_id_type=pl.DeviceIdType.MESH,
        )

    pending = []

    def start(copy):
        copy.start()
        pending.append(copy)

    slots = [(k, e) for k in range(INNER) for e in range(pairs)]

    barrier = pltpu.get_barrier_semaphore()
    greeted = 0
    for m in range(1, outer):
        pl.semaphore_signal(
            barrier,
            inc=1,
            device_id={"ctx": ctx_of(outer_of(m), i_me), "dp": pair},
            device_id_type=pl.DeviceIdType.MESH,
        )
        greeted += 1
    for k, e in slots[1:]:
        pl.semaphore_signal(
            barrier,
            inc=1,
            device_id={"ctx": ctx_of(o_me, inner_of(k)), "dp": (pair + e) % pairs},
            device_id_type=pl.DeviceIdType.MESH,
        )
        greeted += 1
    for s in range(seqs):
        kv[s, me, :, 0:head] = k_ref[s]
        kv[s, me, :, head : 2 * head] = v_ref[s]
    pl.semaphore_wait(barrier, greeted)

    for s in range(seqs):
        for m in range(1, outer):
            start(
                copy_to(
                    kv.at[s, me],
                    kv.at[s, me],
                    ag_send.at[s, m - 1],
                    ag_recv.at[s, me],
                    ctx_of(outer_of(m), i_me),
                    pair,
                )
            )
        for k in range(1, INNER):
            start(
                copy_to(
                    kv.at[s, me],
                    kv.at[s, me],
                    ag_send.at[s, outer - 1 + k - 1],
                    ag_recv.at[s, me],
                    ctx_of(o_me, inner_of(k)),
                    pair,
                )
            )

    def arrived(s, src):
        copy_to(
            kv.at[s, src], kv.at[s, src], ag_send.at[s, 0], ag_recv.at[s, src], me, pair
        ).wait_recv()

    def forward(s):
        for m in range(1, outer):
            src = ctx_of(outer_of(outer - m), i_me)
            arrived(s, src)
            for k in range(1, INNER):
                start(
                    copy_to(
                        kv.at[s, src],
                        kv.at[s, src],
                        ag_send.at[s, outer - 1 + 3 * m + k - 1],
                        ag_recv.at[s, src],
                        ctx_of(o_me, inner_of(k)),
                        pair,
                    )
                )

    def columns_of(row):
        return jnp.broadcast_to(row, (LANES, LANES)).T

    def query_rows(s):
        total = kpos.shape[1] * rows
        per = LANES // rows
        for b in range(total // LANES):
            cut = slice(b * LANES, (b + 1) * LANES)
            pos_col = columns_of(pos_ref[s : s + 1, cut].astype(jnp.float32))
            kpos[s, b * per : (b + 1) * per] = pos_col.reshape(per, rows, LANES)
            dcol[s, cut] = columns_of(doc_ref[s : s + 1, cut].astype(jnp.float32))
        doc_cols = dcol[s]
        place = lax.broadcasted_iota(jnp.int32, (total, LANES), 0).astype(jnp.float32)
        sub = lax.broadcasted_iota(jnp.int32, (step, LANES), 0)
        lane = lax.broadcasted_iota(jnp.int32, (step, LANES), 1)
        pick = sub == lane % step
        found = []
        for g in range(groups):
            own = kpos[s, me, g * step : (g + 1) * step, :]
            pos = jnp.sum(jnp.where(pick, own, 0.0), axis=0, keepdims=True)
            doc = jnp.sum(jnp.where(place == pos, doc_cols, 0.0), axis=0, keepdims=True)
            first = jnp.sum(jnp.where(doc_cols < doc, 1.0, 0.0), axis=0, keepdims=True)
            product = heads_of(g_ref, s, g).astype(jnp.float32) * heads_of(a_ref, s, g).astype(
                jnp.float32
            )
            delta = jnp.sum(product.T, axis=0, keepdims=True)
            found.append((pos, first, delta))
        return found

    def heads_of(ref, s, g):
        return jnp.concatenate(
            [
                ref[s, g * step : (g + 1) * step, h * head : (h + 1) * head]
                for h in range(heads)
            ],
            axis=0,
        )

    def dot(a, b, ca, cb):
        return lax.dot_general(
            a, b, (((ca,), (cb,)), ((), ())), preferred_element_type=jnp.float32
        )

    def attend(s, g, found):
        pos, first, delta = found
        low, high = max(g - 1, 0) * step, (g + 1) * step
        key_count = kpos.shape[1] * (high - low)
        key_block = kv[s, :, low:high, 0:head].reshape(key_count, head)
        value_block = kv[s, :, low:high, head : 2 * head].reshape(key_count, head)
        key_pos = kpos[s, :, low:high, :].reshape(key_count, LANES)
        query_n, grad_n = heads_of(q_ref, s, g), heads_of(g_ref, s, g)
        live = (key_pos <= pos) & (key_pos >= first)
        scores = jnp.where(live, dot(key_block, query_n, 1, 1) * scale, NEG_FILL)
        terms = jnp.exp(scores - jnp.max(scores, axis=0, keepdims=True))
        probs = terms * (1.0 / jnp.sum(terms, axis=0, keepdims=True))
        prob_grad = dot(value_block, grad_n, 1, 1)
        score_grad = (probs * (prob_grad - delta)).astype(jnp.bfloat16)
        value_grad = dot(probs.astype(jnp.bfloat16), grad_n, 1, 0)
        key_grad = dot(score_grad, query_n, 1, 0) * scale
        query_grad = dot(score_grad, key_block, 0, 0) * scale
        for h in range(heads):
            dq_ref[s, g * step : (g + 1) * step, h * head : (h + 1) * head] = query_grad[
                h * step : (h + 1) * step
            ].astype(dq_ref.dtype)
        span = high - low
        shape = (outer, INNER, span, head)
        for part, grad in ((0, key_grad), (1, value_grad)):
            grad = grad.reshape(shape)
            cols = slice(part * head, (part + 1) * head)
            if span > step:
                acc[s, :, :, low : low + step, cols] += grad[:, :, :step]
            acc[s, :, :, high - step : high, cols] = grad[:, :, span - step :]

    def plane_start(s):
        for k in range(1, INNER):
            plane_out[s, k - 1] = acc[s, :, inner_of(k)].astype(jnp.bfloat16)
            start(
                copy_to(
                    plane_out.at[s, k - 1],
                    plane_in.at[s, k - 1],
                    plane_send.at[s, k - 1],
                    plane_recv.at[s, k - 1],
                    ctx_of(o_me, inner_of(k)),
                    pair,
                )
            )

    def outer_start(s):
        total = acc[s, :, i_me]
        for k in range(1, INNER):
            copy_to(
                plane_out.at[s, k - 1],
                plane_in.at[s, k - 1],
                plane_send.at[s, k - 1],
                plane_recv.at[s, k - 1],
                me,
                pair,
            ).wait_recv()
            total += plane_in[s, k - 1].astype(jnp.float32)
        plane_sum[s] = total
        for m in range(1, outer):
            outer_out[s, m - 1] = plane_sum[s, outer_of(m)].astype(jnp.bfloat16)
            start(
                copy_to(
                    outer_out.at[s, m - 1],
                    outer_in.at[s, m - 1],
                    outer_send.at[s, m - 1],
                    outer_recv.at[s, m - 1],
                    ctx_of(outer_of(m), i_me),
                    pair,
                )
            )

    def kvg_start(s):
        total = plane_sum[s, o_me]
        for m in range(1, outer):
            copy_to(
                outer_out.at[s, m - 1],
                outer_in.at[s, m - 1],
                outer_send.at[s, m - 1],
                outer_recv.at[s, m - 1],
                me,
                pair,
            ).wait_recv()
            total += outer_in[s, m - 1].astype(jnp.float32)
        cut = slice(s * rows, (s + 1) * rows)
        kvg[0, cut] = total.astype(jnp.bfloat16)
        for n, (k, e) in enumerate(slots[1:], 1):
            start(
                copy_to(
                    kvg.at[0, cut],
                    kvg.at[n, cut],
                    kvg_send.at[s, n - 1],
                    kvg_recv.at[s, n - 1],
                    ctx_of(o_me, inner_of(k)),
                    (pair + e) % pairs,
                )
            )

    def x_source(o, i, d):
        if x_ref.ndim == 2:
            first = (ctx_of(o, i) * pairs + d) * width
            return x_ref.at[:, pl.ds(pl.multiple_of(first, LANES), width)]
        return x_ref.at[i * pairs + d]

    def x_target(n, o):
        return xg.at[n, o] if x_ref.ndim == 2 else xg.at[n]

    found = []
    for s in range(seqs):
        found.append(query_rows(s))
        forward(s)

    own_copies = []
    for o in range(x_parts):
        own_copies.append(
            pltpu.make_async_copy(x_source(o, i_me, pair), x_target(0, o), own_sem.at[o])
        )
        own_copies[-1].start()
    for n, (k, e) in enumerate(slots[1:], 1):
        for o in range(x_parts):
            start(
                copy_to(
                    x_source(o, inner_of(k), (pair + e) % pairs),
                    x_target(n, o),
                    x_send.at[n - 1, o],
                    x_recv.at[n - 1, o],
                    ctx_of(o_me, inner_of(k)),
                    (pair + e) % pairs,
                )
            )

    for s in range(seqs):
        for k in range(1, INNER):
            for o in range(outer):
                arrived(s, ctx_of(outer_of(o), inner_of(k)))
        for g in range(groups):
            attend(s, g, found[s][g])
        plane_start(s)
    for s in range(seqs):
        outer_start(s)
    for s in range(seqs):
        kvg_start(s)

    for copy in own_copies:
        copy.wait()
    for n, (k, e) in enumerate(slots[1:], 1):
        for o in range(x_parts):
            copy_to(
                x_source(o, i_me, pair),
                x_target(n, o),
                x_send.at[n - 1, o],
                x_recv.at[n - 1, o],
                me,
                pair,
            ).wait_recv()
    for s in range(seqs):
        cut = slice(s * rows, (s + 1) * rows)
        for n in range(1, len(slots)):
            copy_to(
                kvg.at[0, cut],
                kvg.at[n, cut],
                kvg_send.at[s, n - 1],
                kvg_recv.at[s, n - 1],
                me,
                pair,
            ).wait_recv()

    depth = len(slots) * seqs * rows
    kv_grads = kvg[...].reshape(depth, 2 * head)
    for o in range(outer):
        wsum[o] = dot(xg[:, o].reshape(depth, xg.shape[3]), kv_grads, 0, 0)
    for m in range(1, outer):
        w_out[m - 1] = wsum[outer_of(m)].astype(jnp.bfloat16)
        start(
            copy_to(
                w_out.at[m - 1],
                w_in.at[m - 1],
                w_send.at[m - 1],
                w_recv.at[m - 1],
                ctx_of(outer_of(m), i_me),
                pair,
            )
        )
    total = wsum[o_me]
    for m in range(1, outer):
        copy_to(
            w_out.at[m - 1], w_in.at[m - 1], w_send.at[m - 1], w_recv.at[m - 1], me, pair
        ).wait_recv()
        total += w_in[m - 1].astype(jnp.float32)
    w_fin[pair] = total[:width]
    for e in range(1, pairs):
        start(
            copy_to(
                w_fin.at[pair],
                w_fin.at[pair],
                fin_send.at[e - 1],
                fin_recv.at[e - 1],
                me,
                (pair + e) % pairs,
            )
        )
    for e in range(1, pairs):
        src = (pair + pairs - e) % pairs
        copy_to(
            w_fin.at[src], w_fin.at[src], fin_send.at[e - 1], fin_recv.at[e - 1], me, pair
        ).wait_recv()
    dw_ref[...] = w_fin[...].reshape(dw_ref.shape)
    for copy in pending:
        copy.wait_send()


def local(
    layer_input, queries, key_states, value_states, attn_output, out_grad, doc_ids, positions
):
    seqs, rows, model = layer_input.shape
    head = key_states.shape[2]
    ctx = lax.axis_size("ctx")
    pairs = lax.axis_size("dp")
    outer = ctx // INNER
    width = model // (ctx * pairs)
    padded = -(-width // LANES) * LANES
    slots = INNER * pairs
    flat_rows = seqs * rows
    flat = layer_input.reshape(flat_rows, model)
    if padded == width:
        x_parts = outer
    else:
        x_parts = 1
        flat = flat.reshape(flat_rows, outer, INNER * pairs, width).transpose(2, 1, 0, 3)
        flat = jnp.pad(flat, ((0, 0), (0, 0), (0, 0), (0, padded - width)))
    vmem = pl.BlockSpec(memory_space=pltpu.VMEM)
    both = 2 * head
    sends = (outer - 1) + (INNER - 1) + (INNER - 1) * (outer - 1)
    dma = pltpu.SemaphoreType.DMA
    f32, bf16 = jnp.float32, jnp.bfloat16
    return pl.pallas_call(
        functools.partial(kernel, (outer, pairs, width)),
        out_shape=(
            jax.ShapeDtypeStruct(queries.shape, bf16),
            jax.ShapeDtypeStruct((model // ctx, both), f32),
        ),
        in_specs=[pl.BlockSpec(memory_space=pl.ANY)] + [vmem] * 7,
        out_specs=(vmem, vmem),
        scratch_shapes=[
            pltpu.VMEM((seqs, ctx, rows, both), bf16),
            pltpu.VMEM((seqs, ctx, rows, LANES), f32),
            pltpu.VMEM((seqs, ctx * rows, LANES), f32),
            pltpu.VMEM((seqs, outer, INNER, rows, both), f32),
            pltpu.VMEM((seqs, INNER - 1, outer, rows, both), bf16),
            pltpu.VMEM((seqs, INNER - 1, outer, rows, both), bf16),
            pltpu.VMEM((seqs, outer, rows, both), f32),
            pltpu.VMEM((seqs, outer - 1, rows, both), bf16),
            pltpu.VMEM((seqs, outer - 1, rows, both), bf16),
            pltpu.VMEM((slots, flat_rows, both), bf16),
            pltpu.VMEM((slots, outer, flat_rows, padded), bf16),
            pltpu.VMEM((outer, padded, both), f32),
            pltpu.VMEM((outer - 1, padded, both), bf16),
            pltpu.VMEM((outer - 1, padded, both), bf16),
            pltpu.VMEM((pairs, width, both), f32),
            dma((seqs, sends)),
            dma((seqs, ctx)),
            dma((seqs, INNER - 1)),
            dma((seqs, INNER - 1)),
            dma((seqs, outer - 1)),
            dma((seqs, outer - 1)),
            dma((seqs, slots - 1)),
            dma((seqs, slots - 1)),
            dma((slots - 1, x_parts)),
            dma((slots - 1, x_parts)),
            dma((outer - 1,)),
            dma((outer - 1,)),
            dma((pairs - 1,)),
            dma((pairs - 1,)),
            dma((x_parts,)),
        ],
        compiler_params=pltpu.CompilerParams(
            collective_id=0, has_side_effects=True, vmem_limit_bytes=60 * 1024 * 1024
        ),
    )(flat, queries, key_states, value_states, attn_output, out_grad, doc_ids, positions)


def solution(mesh):
    in_specs = (
        P("dp", "ctx", None),
        P("dp", "ctx", None),
        P("dp", "ctx", None),
        P("dp", "ctx", None),
        P("dp", "ctx", None),
        P("dp", "ctx", None),
        P("dp", None),
        P("dp", None),
    )
    out_specs = (P("dp", "ctx", None), P("ctx", None))
    return jax.shard_map(local, mesh=mesh, in_specs=in_specs, out_specs=out_specs, check_vma=False)
```

```python
import functools
import math

import jax
import jax.numpy as jnp
from jax import lax
from jax.experimental import pallas as pl
from jax.experimental.pallas import tpu as pltpu
from jax.sharding import PartitionSpec as P

NEG_FILL = -1e30
INNER = 4
LANES = 128


GROUPS = 4
HALVES = 2


def kernel(
    dims,
    x_ref,
    q_ref,
    k_ref,
    v_ref,
    a_ref,
    g_ref,
    doc_ref,
    pos_ref,
    dq_ref,
    dw_ref,
    kv,
    kv_swap,
    q_in,
    g_in,
    delta_own,
    delta_out,
    delta_in,
    dq_out,
    dq_in,
    kpos,
    dcol,
    acc,
    y_out,
    y_in,
    y_sum,
    z_out,
    z_in,
    z_sum,
    kvg,
    xg,
    wsum,
    w_out,
    w_in,
    w_fin,
    send_sem,
    swap_recv,
    ag_recv,
    y_recv,
    z_recv,
    kvg_recv,
    x_recv,
    w_recv,
    fin_recv,
    own_sem,
):
    outer, pairs, width = dims
    seqs, rows, head = k_ref.shape
    heads = q_ref.shape[2] // head
    step = rows // GROUPS
    scale = 1.0 / math.sqrt(head)
    x_parts = outer if x_ref.ndim == 2 else 1
    ctx_count = outer * INNER

    me = lax.axis_index("ctx")
    pair = lax.axis_index("dp")
    o_me, i_me = me // INNER, me % INNER
    col, row = i_me % 2, i_me // 2
    other = (col + 1) % 2

    def inner_of(k):
        return ((row + k // 2) % 2) * 2 + (col + k % 2) % 2

    def outer_of(m):
        return (o_me + m) % outer

    def ctx_of(o, i):
        return o * INNER + i

    side, across = ctx_of(o_me, inner_of(1)), ctx_of(o_me, inner_of(2))

    pending = []

    def copy_to(src, dst, recv_sem, ctx, dp, slot):
        return pltpu.make_async_remote_copy(
            src_ref=src,
            dst_ref=dst,
            send_sem=send_sem.at[slot],
            recv_sem=recv_sem,
            device_id={"ctx": ctx, "dp": dp},
            device_id_type=pl.DeviceIdType.MESH,
        )

    def send(src, dst, recv_sem, ctx, dp):
        copy = copy_to(src, dst, recv_sem, ctx, dp, len(pending))
        copy.start()
        pending.append(copy)

    def landed(dst, recv_sem):
        copy_to(dst, dst, recv_sem, side, pair, 0).wait_recv()

    slots = [(k, e) for k in range(INNER) for e in range(pairs)]

    barrier = pltpu.get_barrier_semaphore()
    greeted = [(ctx_of(outer_of(m), i_me), pair) for m in range(1, outer)]
    greeted += [(ctx_of(o_me, inner_of(k)), (pair + e) % pairs) for k, e in slots[1:]]
    for ctx, dp in greeted:
        pl.semaphore_signal(
            barrier,
            inc=1,
            device_id={"ctx": ctx, "dp": dp},
            device_id_type=pl.DeviceIdType.MESH,
        )

    def heads_of(block):
        return jnp.concatenate(
            [block[:, h * head : (h + 1) * head] for h in range(heads)], axis=0
        )

    def delta_rows(s, g):
        cut = slice(g * step, (g + 1) * step)
        product = heads_of(g_ref[s, cut, :].astype(jnp.float32)) * heads_of(
            a_ref[s, cut, :].astype(jnp.float32)
        )
        return jnp.sum(product.T, axis=0, keepdims=True)

    kv[me, :, 0:head] = k_ref[col]
    kv[me, :, head : 2 * head] = v_ref[col]
    kv_swap[:, 0:head] = k_ref[other]
    kv_swap[:, head : 2 * head] = v_ref[other]
    pl.semaphore_wait(barrier, len(greeted))

    def half(h):
        return pl.ds(h * (rows // HALVES), rows // HALVES)

    def block_send(src, h, ctx):
        send(kv.at[src, half(h)], kv.at[src, half(h)], ag_recv.at[h, src], ctx, pair)

    def block_landed(src, h):
        landed(kv.at[src, half(h)], ag_recv.at[h, src])

    for h in range(HALVES):
        send(kv_swap.at[half(h)], kv.at[me, half(h)], ag_recv.at[h, me], side, pair)
        for m in range(1, outer):
            block_send(me, h, ctx_of(outer_of(m), i_me))
        block_send(me, h, across)
    send(q_ref.at[other], q_in, swap_recv.at[0], side, pair)
    send(g_ref.at[other], g_in, swap_recv.at[1], side, pair)
    for h in range(HALVES):
        block_landed(side, h)
        for m in range(1, outer):
            block_send(side, h, ctx_of(outer_of(m), i_me))
        block_send(side, h, across)

    for g in range(GROUPS):
        delta_out[g : g + 1, :] = delta_rows(other, g)
    send(delta_out, delta_in, swap_recv.at[2], side, pair)
    for g in range(GROUPS):
        delta_own[g : g + 1, :] = delta_rows(col, g)

    def columns_of(line):
        return jnp.broadcast_to(line, (LANES, LANES)).T

    total_rows = ctx_count * rows
    per = LANES // rows
    pos_line = pos_ref[pl.ds(col, 1), :].astype(jnp.float32)
    doc_line = doc_ref[pl.ds(col, 1), :].astype(jnp.float32)
    for b in range(total_rows // LANES):
        cut = slice(b * LANES, (b + 1) * LANES)
        kpos[b * per : (b + 1) * per] = columns_of(pos_line[:, cut]).reshape(per, rows, LANES)
        dcol[cut] = columns_of(doc_line[:, cut])

    def forward(h):
        for m in range(1, outer):
            o = outer_of(outer - m)
            for src in (ctx_of(o, i_me), ctx_of(o, inner_of(1))):
                block_landed(src, h)
                block_send(src, h, across)

    forward(0)

    place = lax.broadcasted_iota(jnp.int32, (total_rows, LANES), 0).astype(jnp.float32)
    sub = lax.broadcasted_iota(jnp.int32, (step, LANES), 0)
    lane = lax.broadcasted_iota(jnp.int32, (step, LANES), 1)
    pick = sub == lane % step
    doc_cols = dcol[...]

    def query_row(g, src):
        own = kpos[src, g * step : (g + 1) * step, :]
        pos = jnp.sum(jnp.where(pick, own, 0.0), axis=0, keepdims=True)
        doc = jnp.sum(jnp.where(place == pos, doc_cols, 0.0), axis=0, keepdims=True)
        first = jnp.sum(jnp.where(doc_cols < doc, 1.0, 0.0), axis=0, keepdims=True)
        return pos, first

    found = []
    for g in range(GROUPS):
        own_row, side_row = query_row(g, me), query_row(g, side)
        found.append(
            tuple(jnp.concatenate([a, b], axis=1) for a, b in zip(own_row, side_row))
        )
    forward(1)

    def x_source(o, i, d):
        if x_ref.ndim == 2:
            first = (ctx_of(o, i) * pairs + d) * width
            return x_ref.at[:, pl.ds(pl.multiple_of(first, LANES), width)]
        return x_ref.at[i * pairs + d]

    def x_target(n, o):
        return xg.at[n, o] if x_ref.ndim == 2 else xg.at[n]

    own_copies = []
    for o in range(x_parts):
        own_copies.append(
            pltpu.make_async_copy(x_source(o, i_me, pair), x_target(0, o), own_sem.at[o])
        )
        own_copies[-1].start()

    def x_start(chosen):
        for n, (k, e) in enumerate(slots):
            if n and k == chosen:
                for o in range(x_parts):
                    send(
                        x_source(o, inner_of(k), (pair + e) % pairs),
                        x_target(n, o),
                        x_recv.at[n - 1, o],
                        ctx_of(o_me, inner_of(k)),
                        (pair + e) % pairs,
                    )

    def dot(a, b, ca, cb):
        return lax.dot_general(
            a, b, (((ca,), (cb,)), ((), ())), preferred_element_type=jnp.float32
        )

    def attend(g):
        pos, first = found[g]
        low, high = max(g - 1, 0) * step, (g + 1) * step
        span = high - low
        key_count = ctx_count * span
        cut = slice(g * step, (g + 1) * step)
        key_block = kv[:, low:high, 0:head].reshape(key_count, head)
        value_block = kv[:, low:high, head : 2 * head].reshape(key_count, head)
        key_pos = kpos[:, low:high, :].reshape(key_count, LANES)
        key_pos = jnp.concatenate([key_pos, key_pos], axis=1)
        query_n = jnp.concatenate(
            [heads_of(q_ref[col, cut, :]), heads_of(q_in[cut, :])], axis=0
        )
        grad_n = jnp.concatenate(
            [heads_of(g_ref[col, cut, :]), heads_of(g_in[cut, :])], axis=0
        )
        delta = jnp.concatenate([delta_own[g : g + 1, :], delta_in[g : g + 1, :]], axis=1)
        live = (key_pos <= pos) & (key_pos >= first)
        scores = jnp.where(live, dot(key_block, query_n, 1, 1) * scale, NEG_FILL)
        terms = jnp.exp(scores - jnp.max(scores, axis=0, keepdims=True))
        probs = terms * (1.0 / jnp.sum(terms, axis=0, keepdims=True))
        prob_grad = dot(value_block, grad_n, 1, 1)
        score_grad = (probs * (prob_grad - delta)).astype(jnp.bfloat16)
        value_grad = dot(probs.astype(jnp.bfloat16), grad_n, 1, 0)
        key_grad = dot(score_grad, query_n, 1, 0) * scale
        query_grad = (dot(score_grad, key_block, 0, 0) * scale).astype(jnp.bfloat16)
        for h in range(heads):
            cols = slice(h * head, (h + 1) * head)
            dq_ref[col, cut, cols] = query_grad[h * step : (h + 1) * step]
            dq_out[cut, cols] = query_grad[(heads + h) * step : (heads + h + 1) * step]
        for part, grad in ((0, key_grad), (1, value_grad)):
            grad = grad.reshape(outer, 2, 2, span, head)
            cols = slice(part * head, (part + 1) * head)
            if span > step:
                acc[g - 1, :, :, :, :, cols] += grad[:, :, :, :step]
            acc[g, :, :, :, :, cols] = grad[:, :, :, span - step :]

    def y_start(b):
        y_out[b] = acc[b, :, (row + 1) % 2].astype(jnp.bfloat16)
        send(y_out.at[b], y_in.at[b], y_recv.at[b], across, pair)

    def z_start(b):
        landed(y_in.at[b], y_recv.at[b])
        y_sum[b] = acc[b, :, row] + y_in[b].astype(jnp.float32)
        for m in range(1, outer):
            z_out[b, m - 1] = y_sum[b, outer_of(m)].astype(jnp.bfloat16)
            send(
                z_out.at[b, m - 1],
                z_in.at[b, m - 1],
                z_recv.at[b, m - 1],
                ctx_of(outer_of(m), i_me),
                pair,
            )

    def z_finish(b):
        total = y_sum[b, o_me]
        for m in range(1, outer):
            landed(z_in.at[b, m - 1], z_recv.at[b, m - 1])
            total += z_in[b, m - 1].astype(jnp.float32)
        z_sum[:, b * step : (b + 1) * step, :] = total.astype(jnp.bfloat16)

    def wait_half(h):
        for o in range(outer):
            for k in (2, 3):
                block_landed(ctx_of(outer_of(o), inner_of(k)), h)

    x_start(0)
    wait_half(0)
    landed(q_in, swap_recv.at[0])
    landed(g_in, swap_recv.at[1])
    landed(delta_in, swap_recv.at[2])
    x_start(1)
    for g in range(GROUPS):
        if g == GROUPS // HALVES:
            wait_half(1)
            x_start(2)
        attend(g)
        if g >= 1:
            y_start(g - 1)
        if g >= 2:
            z_start(g - 2)
    y_start(GROUPS - 1)
    send(dq_out, dq_in, swap_recv.at[3], side, pair)
    z_start(GROUPS - 2)
    z_start(GROUPS - 1)
    x_start(3)
    for b in range(GROUPS):
        z_finish(b)

    def kvg_at(k, e, s):
        return kvg.at[k * pairs + e, s], kvg_recv.at[k * pairs + e, s]

    def pass_on(k, s):
        for e in range(1, pairs):
            dst, recv_sem = kvg_at(k, e, s)
            send(kvg_at(k, 0, s)[0], dst, recv_sem, me, (pair + e) % pairs)

    for k in range(1, INNER):
        for b in range(2):
            dst, recv_sem = kvg_at(k // 2 * 2 + b, 0, col)
            send(
                z_sum.at[(col + k + b) % 2],
                dst,
                recv_sem,
                ctx_of(o_me, inner_of(k)),
                pair,
            )
    for b in range(2):
        kvg[b * pairs, col] = z_sum[(col + b) % 2]
        pass_on(b, col)
    for b in range(2):
        landed(*kvg_at(b, 0, other))
        pass_on(b, other)
    for b in (2, 3):
        for s in range(seqs):
            landed(*kvg_at(b, 0, s))
            pass_on(b, s)

    landed(dq_in, swap_recv.at[3])
    dq_ref[other] = dq_in[...]
    for copy in own_copies:
        copy.wait()
    for n in range(1, len(slots)):
        for o in range(x_parts):
            landed(x_target(n, o), x_recv.at[n - 1, o])
    for k in range(INNER):
        for e in range(1, pairs):
            for s in range(seqs):
                landed(*kvg_at(k, e, s))

    depth = len(slots) * seqs * rows
    kv_grads = kvg[...].reshape(depth, 2 * head)
    for o in range(outer):
        wsum[o] = dot(xg[:, o].reshape(depth, xg.shape[3]), kv_grads, 0, 0)
    for m in range(1, outer):
        w_out[m - 1] = wsum[outer_of(m)].astype(jnp.bfloat16)
        send(
            w_out.at[m - 1], w_in.at[m - 1], w_recv.at[m - 1], ctx_of(outer_of(m), i_me), pair
        )
    total = wsum[o_me]
    for m in range(1, outer):
        landed(w_in.at[m - 1], w_recv.at[m - 1])
        total += w_in[m - 1].astype(jnp.float32)
    w_fin[pair] = total[:width]
    for e in range(1, pairs):
        send(w_fin.at[pair], w_fin.at[pair], fin_recv.at[e - 1], me, (pair + e) % pairs)
    for e in range(1, pairs):
        landed(w_fin.at[(pair + pairs - e) % pairs], fin_recv.at[e - 1])
    dw_ref[...] = w_fin[...].reshape(dw_ref.shape)
    for copy in pending:
        copy.wait_send()


def local(
    layer_input, queries, key_states, value_states, attn_output, out_grad, doc_ids, positions
):
    seqs, rows, model = layer_input.shape
    head = key_states.shape[2]
    ctx = lax.axis_size("ctx")
    pairs = lax.axis_size("dp")
    outer = ctx // INNER
    width = model // (ctx * pairs)
    padded = -(-width // LANES) * LANES
    slots = INNER * pairs
    flat_rows = seqs * rows
    flat = layer_input.reshape(flat_rows, model)
    if padded == width:
        x_parts = outer
    else:
        x_parts = 1
        flat = flat.reshape(flat_rows, outer, INNER * pairs, width).transpose(2, 1, 0, 3)
        flat = jnp.pad(flat, ((0, 0), (0, 0), (0, 0), (0, padded - width)))
    vmem = pl.BlockSpec(memory_space=pltpu.VMEM)
    both = 2 * head
    sends = HALVES * (4 * outer + 1) + 4 + GROUPS * outer + 6 + 8 * (pairs - 1)
    sends += (slots - 1) * x_parts + (outer - 1) + (pairs - 1)
    dma = pltpu.SemaphoreType.DMA
    f32, bf16 = jnp.float32, jnp.bfloat16
    step = rows // GROUPS
    query_width = queries.shape[2]
    return pl.pallas_call(
        functools.partial(kernel, (outer, pairs, width)),
        out_shape=(
            jax.ShapeDtypeStruct(queries.shape, bf16),
            jax.ShapeDtypeStruct((model // ctx, both), f32),
        ),
        in_specs=[pl.BlockSpec(memory_space=pl.ANY)] + [vmem] * 7,
        out_specs=(vmem, vmem),
        scratch_shapes=[
            pltpu.VMEM((ctx, rows, both), bf16),
            pltpu.VMEM((rows, both), bf16),
            pltpu.VMEM((rows, query_width), bf16),
            pltpu.VMEM((rows, query_width), bf16),
            pltpu.VMEM((8, LANES), f32),
            pltpu.VMEM((8, LANES), f32),
            pltpu.VMEM((8, LANES), f32),
            pltpu.VMEM((rows, query_width), bf16),
            pltpu.VMEM((rows, query_width), bf16),
            pltpu.VMEM((ctx, rows, LANES), f32),
            pltpu.VMEM((ctx * rows, LANES), f32),
            pltpu.VMEM((GROUPS, outer, 2, 2, step, both), f32),
            pltpu.VMEM((GROUPS, outer, 2, step, both), bf16),
            pltpu.VMEM((GROUPS, outer, 2, step, both), bf16),
            pltpu.VMEM((GROUPS, outer, 2, step, both), f32),
            pltpu.VMEM((GROUPS, outer - 1, 2, step, both), bf16),
            pltpu.VMEM((GROUPS, outer - 1, 2, step, both), bf16),
            pltpu.VMEM((2, rows, both), bf16),
            pltpu.VMEM((slots, seqs, rows, both), bf16),
            pltpu.VMEM((slots, outer, flat_rows, padded), bf16),
            pltpu.VMEM((outer, padded, both), f32),
            pltpu.VMEM((outer - 1, padded, both), bf16),
            pltpu.VMEM((outer - 1, padded, both), bf16),
            pltpu.VMEM((pairs, width, both), f32),
            dma((sends,)),
            dma((4,)),
            dma((HALVES, ctx)),
            dma((GROUPS,)),
            dma((GROUPS, outer - 1)),
            dma((slots, seqs)),
            dma((slots - 1, x_parts)),
            dma((outer - 1,)),
            dma((pairs - 1,)),
            dma((x_parts,)),
        ],
        compiler_params=pltpu.CompilerParams(
            collective_id=0, has_side_effects=True, vmem_limit_bytes=60 * 1024 * 1024
        ),
    )(flat, queries, key_states, value_states, attn_output, out_grad, doc_ids, positions)


def solution(mesh):
    in_specs = (
        P("dp", "ctx", None),
        P("dp", "ctx", None),
        P("dp", "ctx", None),
        P("dp", "ctx", None),
        P("dp", "ctx", None),
        P("dp", "ctx", None),
        P("dp", None),
        P("dp", None),
    )
    out_specs = (P("dp", "ctx", None), P("ctx", None))
    return jax.shard_map(local, mesh=mesh, in_specs=in_specs, out_specs=out_specs, check_vma=False)
```

```python
import functools
import math

import jax
import jax.numpy as jnp
from jax import lax
from jax.experimental import pallas as pl
from jax.experimental.pallas import tpu as pltpu
from jax.sharding import PartitionSpec as P

NEG_FILL = -1e30
INNER = 4
LANES = 128


GROUPS = 4
HALVES = 2


def kernel(
    dims,
    x_ref,
    q_ref,
    k_ref,
    v_ref,
    a_ref,
    g_ref,
    doc_ref,
    pos_ref,
    dq_ref,
    dw_ref,
    kv,
    kv_swap,
    q_in,
    g_in,
    delta_own,
    delta_out,
    delta_in,
    dq_out,
    dq_in,
    kpos,
    dcol,
    acc,
    y_out,
    y_in,
    y_sum,
    z_out,
    z_in,
    z_sum,
    kvg,
    xg,
    xt,
    wsum,
    w_out,
    w_in,
    w_fin,
    send_sem,
    swap_recv,
    side_recv,
    ag_recv,
    y_recv,
    z_recv,
    kvg_recv,
    x_recv,
    w_recv,
    fin_recv,
    own_sem,
):
    outer, pairs, width = dims
    seqs, rows, head = k_ref.shape
    heads = q_ref.shape[2] // head
    step = rows // GROUPS
    scale = 1.0 / math.sqrt(head)
    x_parts = outer if x_ref.ndim == 2 else 1
    ctx_count = outer * INNER

    me = lax.axis_index("ctx")
    pair = lax.axis_index("dp")
    o_me, i_me = me // INNER, me % INNER
    col, row = i_me % 2, i_me // 2
    other = (col + 1) % 2

    def inner_of(k):
        return ((row + k // 2) % 2) * 2 + (col + k % 2) % 2

    def outer_of(m):
        return (o_me + m) % outer

    def ctx_of(o, i):
        return o * INNER + i

    side, across = ctx_of(o_me, inner_of(1)), ctx_of(o_me, inner_of(2))

    pending = []

    def copy_to(src, dst, recv_sem, ctx, dp, slot):
        return pltpu.make_async_remote_copy(
            src_ref=src,
            dst_ref=dst,
            send_sem=send_sem.at[slot],
            recv_sem=recv_sem,
            device_id={"ctx": ctx, "dp": dp},
            device_id_type=pl.DeviceIdType.MESH,
        )

    def send(src, dst, recv_sem, ctx, dp):
        copy = copy_to(src, dst, recv_sem, ctx, dp, len(pending))
        copy.start()
        pending.append(copy)

    def landed(dst, recv_sem):
        copy_to(dst, dst, recv_sem, side, pair, 0).wait_recv()

    slots = [(k, e) for k in range(INNER) for e in range(pairs)]

    barrier = pltpu.get_barrier_semaphore()
    greeted = [(ctx_of(outer_of(m), i_me), pair) for m in range(1, outer)]
    greeted += [(ctx_of(o_me, inner_of(k)), (pair + e) % pairs) for k, e in slots[1:]]
    for ctx, dp in greeted:
        pl.semaphore_signal(
            barrier,
            inc=1,
            device_id={"ctx": ctx, "dp": dp},
            device_id_type=pl.DeviceIdType.MESH,
        )

    def heads_of(block):
        return jnp.concatenate(
            [block[:, h * head : (h + 1) * head] for h in range(heads)], axis=0
        )

    def delta_rows(s, g):
        cut = slice(g * step, (g + 1) * step)
        product = heads_of(g_ref[s, cut, :].astype(jnp.float32)) * heads_of(
            a_ref[s, cut, :].astype(jnp.float32)
        )
        return jnp.sum(product.T, axis=0, keepdims=True)

    kv[me, :, 0:head] = k_ref[col]
    kv[me, :, head : 2 * head] = v_ref[col]
    kv_swap[:, 0:head] = k_ref[other]
    kv_swap[:, head : 2 * head] = v_ref[other]
    pl.semaphore_wait(barrier, len(greeted))

    def half(h):
        return pl.ds(h * (rows // HALVES), rows // HALVES)

    def block_send(src, h, ctx):
        send(kv.at[src, half(h)], kv.at[src, half(h)], ag_recv.at[h, src], ctx, pair)

    def block_landed(src, h):
        landed(kv.at[src, half(h)], ag_recv.at[h, src])

    for h in range(HALVES):
        send(kv_swap.at[half(h)], kv.at[me, half(h)], ag_recv.at[h, me], side, pair)
        for m in range(1, outer):
            block_send(me, h, ctx_of(outer_of(m), i_me))
        block_send(me, h, across)
    for g in range(GROUPS):
        cut = pl.ds(g * step, step)
        send(q_ref.at[other, cut], q_in.at[cut], swap_recv.at[g, 0], side, pair)
        send(g_ref.at[other, cut], g_in.at[cut], swap_recv.at[g, 1], side, pair)
    def x_source(o, i, d):
        if x_ref.ndim == 2:
            first = (ctx_of(o, i) * pairs + d) * width
            return x_ref.at[:, pl.ds(pl.multiple_of(first, LANES), width)]
        return x_ref.at[i * pairs + d]

    def x_target(n, o):
        return xg.at[n, o] if x_ref.ndim == 2 else xg.at[n]

    own_copies = []
    for o in range(x_parts):
        own_copies.append(
            pltpu.make_async_copy(x_source(o, i_me, pair), x_target(0, o), own_sem.at[o])
        )
        own_copies[-1].start()

    def x_start(chosen, first=0, last=x_parts):
        for n, (k, e) in enumerate(slots):
            if n and k == chosen:
                for o in range(first, last):
                    send(
                        x_source(o, inner_of(k), (pair + e) % pairs),
                        x_target(n, o),
                        x_recv.at[n - 1, o],
                        ctx_of(o_me, inner_of(k)),
                        (pair + e) % pairs,
                    )

    x_start(0)
    for h in range(HALVES):
        block_landed(side, h)
        for m in range(1, outer):
            block_send(side, h, ctx_of(outer_of(m), i_me))
        block_send(side, h, across)

    for g in range(GROUPS):
        delta_out[g : g + 1, :] = delta_rows(other, g)
    send(delta_out, delta_in, side_recv.at[0], side, pair)
    def forward(h):
        for m in range(1, outer):
            o = outer_of(outer - m)
            for src in (ctx_of(o, i_me), ctx_of(o, inner_of(1))):
                block_landed(src, h)
                block_send(src, h, across)

    forward(0)
    for g in range(GROUPS):
        delta_own[g : g + 1, :] = delta_rows(col, g)

    def columns_of(line):
        return jnp.broadcast_to(line, (LANES, LANES)).T

    total_rows = ctx_count * rows
    per = LANES // rows
    pos_line = pos_ref[pl.ds(col, 1), :].astype(jnp.float32)
    doc_line = doc_ref[pl.ds(col, 1), :].astype(jnp.float32)
    for b in range(total_rows // LANES):
        cut = slice(b * LANES, (b + 1) * LANES)
        kpos[b * per : (b + 1) * per] = columns_of(pos_line[:, cut]).reshape(per, rows, LANES)
        dcol[cut] = columns_of(doc_line[:, cut])

    forward(1)
    place = lax.broadcasted_iota(jnp.int32, (total_rows, LANES), 0).astype(jnp.float32)
    sub = lax.broadcasted_iota(jnp.int32, (step, LANES), 0)
    lane = lax.broadcasted_iota(jnp.int32, (step, LANES), 1)
    pick = sub == lane % step
    doc_cols = dcol[...]

    def query_row(g, src):
        own = kpos[src, g * step : (g + 1) * step, :]
        pos = jnp.sum(jnp.where(pick, own, 0.0), axis=0, keepdims=True)
        doc = jnp.sum(jnp.where(place == pos, doc_cols, 0.0), axis=0, keepdims=True)
        first = jnp.sum(jnp.where(doc_cols < doc, 1.0, 0.0), axis=0, keepdims=True)
        return pos, first

    found = []
    for g in range(GROUPS):
        own_row, side_row = query_row(g, me), query_row(g, side)
        found.append(
            tuple(jnp.concatenate([a, b], axis=1) for a, b in zip(own_row, side_row))
        )

    def dot(a, b, ca, cb):
        return lax.dot_general(
            a, b, (((ca,), (cb,)), ((), ())), preferred_element_type=jnp.float32
        )

    def attend(g):
        pos, first = found[g]
        low, high = max(g - 1, 0) * step, (g + 1) * step
        span = high - low
        key_count = ctx_count * span
        cut = slice(g * step, (g + 1) * step)
        key_block = kv[:, low:high, 0:head].reshape(key_count, head)
        value_block = kv[:, low:high, head : 2 * head].reshape(key_count, head)
        key_pos = kpos[:, low:high, :].reshape(key_count, LANES)
        key_pos = jnp.concatenate([key_pos, key_pos], axis=1)
        query_n = jnp.concatenate(
            [heads_of(q_ref[col, cut, :]), heads_of(q_in[cut, :])], axis=0
        )
        grad_n = jnp.concatenate(
            [heads_of(g_ref[col, cut, :]), heads_of(g_in[cut, :])], axis=0
        )
        delta = jnp.concatenate([delta_own[g : g + 1, :], delta_in[g : g + 1, :]], axis=1)
        live = (key_pos <= pos) & (key_pos >= first)
        scores = jnp.where(live, dot(key_block, query_n, 1, 1) * scale, NEG_FILL)
        terms = jnp.exp(scores - jnp.max(scores, axis=0, keepdims=True))
        probs = terms * (1.0 / jnp.sum(terms, axis=0, keepdims=True))
        prob_grad = dot(value_block, grad_n, 1, 1)
        score_grad = (probs * (prob_grad - delta)).astype(jnp.bfloat16)
        value_grad = dot(probs.astype(jnp.bfloat16), grad_n, 1, 0)
        key_grad = dot(score_grad, query_n, 1, 0) * scale
        query_grad = (dot(score_grad, key_block, 0, 0) * scale).astype(jnp.bfloat16)
        for h in range(heads):
            cols = slice(h * head, (h + 1) * head)
            dq_ref[col, cut, cols] = query_grad[h * step : (h + 1) * step]
            dq_out[cut, cols] = query_grad[(heads + h) * step : (heads + h + 1) * step]
        for part, grad in ((0, key_grad), (1, value_grad)):
            grad = grad.reshape(outer, 2, 2, span, head)
            cols = slice(part * head, (part + 1) * head)
            if span > step:
                acc[g - 1, :, :, :, :, cols] += grad[:, :, :, :step]
            acc[g, :, :, :, :, cols] = grad[:, :, :, span - step :]

    def y_start(b):
        y_out[b] = acc[b, :, (row + 1) % 2].astype(jnp.bfloat16)
        send(y_out.at[b], y_in.at[b], y_recv.at[b], across, pair)

    def z_start(b):
        landed(y_in.at[b], y_recv.at[b])
        y_sum[b] = acc[b, :, row] + y_in[b].astype(jnp.float32)
        for m in range(1, outer):
            z_out[b, m - 1] = y_sum[b, outer_of(m)].astype(jnp.bfloat16)
            send(
                z_out.at[b, m - 1],
                z_in.at[b, m - 1],
                z_recv.at[b, m - 1],
                ctx_of(outer_of(m), i_me),
                pair,
            )

    def z_finish(b):
        total = y_sum[b, o_me]
        for m in range(1, outer):
            landed(z_in.at[b, m - 1], z_recv.at[b, m - 1])
            total += z_in[b, m - 1].astype(jnp.float32)
        z_sum[:, b * step : (b + 1) * step, :] = total.astype(jnp.bfloat16)

    def wait_half(h):
        for o in range(outer):
            for k in (2, 3):
                block_landed(ctx_of(outer_of(o), inner_of(k)), h)

    def kvg_at(k, e, s, h):
        slot = k * pairs + e
        return kvg.at[slot, s, half(h)], kvg_recv.at[h, slot, s]

    def pass_on(k, s, h):
        for e in range(1, pairs):
            dst, recv_sem = kvg_at(k, e, s, h)
            send(kvg_at(k, 0, s, h)[0], dst, recv_sem, me, (pair + e) % pairs)

    def kvg_start(h):
        for k in range(1, INNER):
            for b in range(2):
                dst, recv_sem = kvg_at(k // 2 * 2 + b, 0, col, h)
                send(
                    z_sum.at[(col + k + b) % 2, half(h)],
                    dst,
                    recv_sem,
                    ctx_of(o_me, inner_of(k)),
                    pair,
                )
        for b in range(2):
            kvg[b * pairs, col, half(h)] = z_sum[(col + b) % 2, half(h)]
            pass_on(b, col, h)

    def kvg_forward(h):
        for b in range(2):
            landed(*kvg_at(b, 0, other, h))
            pass_on(b, other, h)
        for b in (2, 3):
            for s in range(seqs):
                landed(*kvg_at(b, 0, s, h))
                pass_on(b, s, h)

    def x_turn(chosen):
        for n, (k, e) in enumerate(slots):
            if k == chosen:
                for o in range(x_parts):
                    if n:
                        landed(x_target(n, o), x_recv.at[n - 1, o])
                    else:
                        own_copies[o].wait()
                cut = slice(n * seqs * rows, (n + 1) * seqs * rows)
                for o in range(outer):
                    xt[o, :, cut] = xg[n, o].T

    x_start(3)
    x_start(1)
    wait_half(0)
    landed(delta_in, side_recv.at[0])
    for g in range(GROUPS):
        cut = pl.ds(g * step, step)
        landed(q_in.at[cut], swap_recv.at[g, 0])
        landed(g_in.at[cut], swap_recv.at[g, 1])
        if g == GROUPS // HALVES:
            wait_half(1)
            x_start(2, 0, (x_parts + 1) // 2)
        attend(g)
        if g >= 1:
            y_start(g - 1)
        if g >= 2:
            z_start(g - 2)
    y_start(GROUPS - 1)
    send(dq_out, dq_in, side_recv.at[1], side, pair)
    x_start(2, (x_parts + 1) // 2)
    z_start(GROUPS - 2)
    z_start(GROUPS - 1)
    x_turn(0)
    z_finish(0)
    z_finish(1)
    kvg_start(0)
    z_finish(2)
    z_finish(3)
    kvg_start(1)
    x_turn(1)
    kvg_forward(0)
    x_turn(3)
    kvg_forward(1)
    x_turn(2)
    landed(dq_in, side_recv.at[1])
    dq_ref[other] = dq_in[...]
    for h in range(HALVES):
        for k in range(INNER):
            for e in range(1, pairs):
                for s in range(seqs):
                    landed(*kvg_at(k, e, s, h))

    depth = len(slots) * seqs * rows
    kv_grads = kvg[...].reshape(depth, 2 * head)
    for m in range(1, outer):
        w_out[m - 1] = dot(xt[outer_of(m)], kv_grads, 1, 0).astype(jnp.bfloat16)
        send(
            w_out.at[m - 1], w_in.at[m - 1], w_recv.at[m - 1], ctx_of(outer_of(m), i_me), pair
        )
    wsum[...] = dot(xt[o_me], kv_grads, 1, 0)
    total = wsum[...]
    for m in range(1, outer):
        landed(w_in.at[m - 1], w_recv.at[m - 1])
        total += w_in[m - 1].astype(jnp.float32)
    w_fin[pair] = total[:width]
    for e in range(1, pairs):
        send(w_fin.at[pair], w_fin.at[pair], fin_recv.at[e - 1], me, (pair + e) % pairs)
    for e in range(1, pairs):
        landed(w_fin.at[(pair + pairs - e) % pairs], fin_recv.at[e - 1])
    dw_ref[...] = w_fin[...].reshape(dw_ref.shape)
    for copy in pending:
        copy.wait_send()


def local(
    layer_input, queries, key_states, value_states, attn_output, out_grad, doc_ids, positions
):
    seqs, rows, model = layer_input.shape
    head = key_states.shape[2]
    ctx = lax.axis_size("ctx")
    pairs = lax.axis_size("dp")
    outer = ctx // INNER
    width = model // (ctx * pairs)
    padded = -(-width // LANES) * LANES
    slots = INNER * pairs
    flat_rows = seqs * rows
    flat = layer_input.reshape(flat_rows, model)
    if padded == width:
        x_parts = outer
    else:
        x_parts = 1
        flat = flat.reshape(flat_rows, outer, INNER * pairs, width).transpose(2, 1, 0, 3)
        flat = jnp.pad(flat, ((0, 0), (0, 0), (0, 0), (0, padded - width)))
    vmem = pl.BlockSpec(memory_space=pltpu.VMEM)
    both = 2 * head
    sends = HALVES * (4 * outer + 1) + 2 * GROUPS + 2 + GROUPS * outer
    sends += HALVES * (6 + 8 * (pairs - 1))
    sends += (slots - 1) * x_parts + (outer - 1) + (pairs - 1)
    dma = pltpu.SemaphoreType.DMA
    f32, bf16 = jnp.float32, jnp.bfloat16
    step = rows // GROUPS
    query_width = queries.shape[2]
    return pl.pallas_call(
        functools.partial(kernel, (outer, pairs, width)),
        out_shape=(
            jax.ShapeDtypeStruct(queries.shape, bf16),
            jax.ShapeDtypeStruct((model // ctx, both), f32),
        ),
        in_specs=[pl.BlockSpec(memory_space=pl.ANY)] + [vmem] * 7,
        out_specs=(vmem, vmem),
        scratch_shapes=[
            pltpu.VMEM((ctx, rows, both), bf16),
            pltpu.VMEM((rows, both), bf16),
            pltpu.VMEM((rows, query_width), bf16),
            pltpu.VMEM((rows, query_width), bf16),
            pltpu.VMEM((8, LANES), f32),
            pltpu.VMEM((8, LANES), f32),
            pltpu.VMEM((8, LANES), f32),
            pltpu.VMEM((rows, query_width), bf16),
            pltpu.VMEM((rows, query_width), bf16),
            pltpu.VMEM((ctx, rows, LANES), f32),
            pltpu.VMEM((ctx * rows, LANES), f32),
            pltpu.VMEM((GROUPS, outer, 2, 2, step, both), f32),
            pltpu.VMEM((GROUPS, outer, 2, step, both), bf16),
            pltpu.VMEM((GROUPS, outer, 2, step, both), bf16),
            pltpu.VMEM((GROUPS, outer, 2, step, both), f32),
            pltpu.VMEM((GROUPS, outer - 1, 2, step, both), bf16),
            pltpu.VMEM((GROUPS, outer - 1, 2, step, both), bf16),
            pltpu.VMEM((2, rows, both), bf16),
            pltpu.VMEM((slots, seqs, rows, both), bf16),
            pltpu.VMEM((slots, outer, flat_rows, padded), bf16),
            pltpu.VMEM((outer, padded, slots * flat_rows), bf16),
            pltpu.VMEM((padded, both), f32),
            pltpu.VMEM((outer - 1, padded, both), bf16),
            pltpu.VMEM((outer - 1, padded, both), bf16),
            pltpu.VMEM((pairs, width, both), f32),
            dma((sends,)),
            dma((GROUPS, 2)),
            dma((2,)),
            dma((HALVES, ctx)),
            dma((GROUPS,)),
            dma((GROUPS, outer - 1)),
            dma((HALVES, slots, seqs)),
            dma((slots - 1, x_parts)),
            dma((outer - 1,)),
            dma((pairs - 1,)),
            dma((x_parts,)),
        ],
        compiler_params=pltpu.CompilerParams(
            collective_id=0, has_side_effects=True, vmem_limit_bytes=60 * 1024 * 1024
        ),
    )(flat, queries, key_states, value_states, attn_output, out_grad, doc_ids, positions)


def solution(mesh):
    in_specs = (
        P("dp", "ctx", None),
        P("dp", "ctx", None),
        P("dp", "ctx", None),
        P("dp", "ctx", None),
        P("dp", "ctx", None),
        P("dp", "ctx", None),
        P("dp", None),
        P("dp", None),
    )
    out_specs = (P("dp", "ctx", None), P("ctx", None))
    return jax.shard_map(local, mesh=mesh, in_specs=in_specs, out_specs=out_specs, check_vma=False)
```

```python
import functools
import math

import jax
import jax.numpy as jnp
from jax import lax
from jax.experimental import pallas as pl
from jax.experimental.pallas import tpu as pltpu
from jax.sharding import PartitionSpec as P

NEG_FILL = -1e30
INNER = 4
LANES = 128


GROUPS = 4
HALVES = 2


def kernel(
    dims,
    x_ref,
    q_ref,
    k_ref,
    v_ref,
    a_ref,
    g_ref,
    doc_ref,
    pos_ref,
    dq_ref,
    dw_ref,
    kv,
    kv_swap,
    q_in,
    g_in,
    delta_own,
    delta_out,
    delta_in,
    dq_out,
    dq_in,
    kpos,
    dcol,
    acc,
    y_out,
    y_in,
    y_sum,
    z_out,
    z_in,
    z_sum,
    kvg,
    xg,
    xt,
    wsum,
    w_out,
    w_in,
    w_fin,
    send_sem,
    swap_recv,
    side_recv,
    kv_recv,
    ag_recv,
    y_recv,
    z_recv,
    kvg_recv,
    x_recv,
    w_recv,
    fin_recv,
    own_sem,
):
    outer, pairs, width = dims
    seqs, rows, head = k_ref.shape
    heads = q_ref.shape[2] // head
    step = rows // GROUPS
    scale = 1.0 / math.sqrt(head)
    x_parts = outer if x_ref.ndim == 2 else 1
    ctx_count = outer * INNER

    me = lax.axis_index("ctx")
    pair = lax.axis_index("dp")
    o_me, i_me = me // INNER, me % INNER
    col, row = i_me % 2, i_me // 2
    other = (col + 1) % 2

    def inner_of(k):
        return ((row + k // 2) % 2) * 2 + (col + k % 2) % 2

    def outer_of(m):
        return (o_me + m) % outer

    def ctx_of(o, i):
        return o * INNER + i

    side, across = ctx_of(o_me, inner_of(1)), ctx_of(o_me, inner_of(2))

    pending = []

    def copy_to(src, dst, recv_sem, ctx, dp, slot):
        return pltpu.make_async_remote_copy(
            src_ref=src,
            dst_ref=dst,
            send_sem=send_sem.at[slot],
            recv_sem=recv_sem,
            device_id={"ctx": ctx, "dp": dp},
            device_id_type=pl.DeviceIdType.MESH,
        )

    def send(src, dst, recv_sem, ctx, dp):
        copy = copy_to(src, dst, recv_sem, ctx, dp, len(pending))
        copy.start()
        pending.append(copy)

    def landed(dst, recv_sem):
        copy_to(dst, dst, recv_sem, side, pair, 0).wait_recv()

    slots = [(k, e) for k in range(INNER) for e in range(pairs)]

    barrier = pltpu.get_barrier_semaphore()
    greeted = [(ctx_of(outer_of(m), i_me), pair) for m in range(1, outer)]
    greeted += [(ctx_of(o_me, inner_of(k)), (pair + e) % pairs) for k, e in slots[1:]]
    for ctx, dp in greeted:
        pl.semaphore_signal(
            barrier,
            inc=1,
            device_id={"ctx": ctx, "dp": dp},
            device_id_type=pl.DeviceIdType.MESH,
        )

    def heads_of(block):
        return jnp.concatenate(
            [block[:, h * head : (h + 1) * head] for h in range(heads)], axis=0
        )

    def delta_rows(s, g):
        cut = slice(g * step, (g + 1) * step)
        product = heads_of(g_ref[s, cut, :].astype(jnp.float32)) * heads_of(
            a_ref[s, cut, :].astype(jnp.float32)
        )
        return jnp.sum(product.T, axis=0, keepdims=True)

    kv[me, :, 0:head] = k_ref[col]
    kv[me, :, head : 2 * head] = v_ref[col]
    kv_swap[:, 0:head] = k_ref[other]
    kv_swap[:, head : 2 * head] = v_ref[other]
    pl.semaphore_wait(barrier, len(greeted))

    def half(h):
        return pl.ds(h * (rows // HALVES), rows // HALVES)

    def both_of(o, r, h):
        blocks = kv.at[pl.ds(ctx_of(o, 2 * r), 2), half(h)]
        return blocks, ag_recv.at[h, o * 2 + r]

    def both_send(o, h, ctx):
        blocks, recv_sem = both_of(o, row, h)
        send(blocks, blocks, recv_sem, ctx, pair)

    for h in range(HALVES):
        send(kv_swap.at[half(h)], kv.at[me, half(h)], kv_recv.at[h], side, pair)
    for g in range(GROUPS):
        cut = pl.ds(g * step, step)
        send(q_ref.at[other, cut], q_in.at[cut], swap_recv.at[g, 0], side, pair)
        send(g_ref.at[other, cut], g_in.at[cut], swap_recv.at[g, 1], side, pair)
    def x_source(o, i, d):
        if x_ref.ndim == 2:
            first = (ctx_of(o, i) * pairs + d) * width
            return x_ref.at[:, pl.ds(pl.multiple_of(first, LANES), width)]
        return x_ref.at[i * pairs + d]

    def slot_of(k, e, column):
        return (e * 2 + k // 2) * 2 + (column + k % 2) % 2

    def x_target(n, o):
        return xg.at[n, o] if x_ref.ndim == 2 else xg.at[n]

    own_copies = []
    for o in range(x_parts):
        own_copies.append(
            pltpu.make_async_copy(x_source(o, i_me, pair), x_target(slot_of(0, 0, col), o), own_sem.at[o])
        )
        own_copies[-1].start()

    def x_start(chosen, first=0, last=x_parts):
        for n, (k, e) in enumerate(slots):
            if n and k == chosen:
                for o in range(first, last):
                    send(
                        x_source(o, inner_of(k), (pair + e) % pairs),
                        x_target(slot_of(k - k % 2, e, col), o),
                        x_recv.at[n - 1, o],
                        ctx_of(o_me, inner_of(k)),
                        (pair + e) % pairs,
                    )

    x_start(0)
    for h in range(HALVES):
        landed(kv.at[side, half(h)], kv_recv.at[h])
        for m in range(1, outer):
            both_send(o_me, h, ctx_of(outer_of(m), i_me))
        both_send(o_me, h, across)

    for g in range(GROUPS):
        delta_out[g : g + 1, :] = delta_rows(other, g)
    send(delta_out, delta_in, side_recv.at[0], side, pair)
    def forward(h):
        for m in range(1, outer):
            o = outer_of(outer - m)
            landed(*both_of(o, row, h))
            both_send(o, h, across)

    forward(0)
    for g in range(GROUPS):
        delta_own[g : g + 1, :] = delta_rows(col, g)

    def columns_of(line):
        return jnp.broadcast_to(line, (LANES, LANES)).T

    total_rows = ctx_count * rows
    per = LANES // rows
    pos_line = pos_ref[pl.ds(col, 1), :].astype(jnp.float32)
    doc_line = doc_ref[pl.ds(col, 1), :].astype(jnp.float32)
    for b in range(total_rows // LANES):
        cut = slice(b * LANES, (b + 1) * LANES)
        kpos[b * per : (b + 1) * per] = columns_of(pos_line[:, cut]).reshape(per, rows, LANES)
        dcol[cut] = columns_of(doc_line[:, cut])

    forward(1)
    own_rows = jnp.concatenate([kpos[me], kpos[side]], axis=0)
    sub = lax.broadcasted_iota(jnp.int32, own_rows.shape, 0)
    lane = lax.broadcasted_iota(jnp.int32, own_rows.shape, 1)
    row_pos = jnp.sum(jnp.where(sub == lane, own_rows, 0.0), axis=0, keepdims=True)
    place = lax.broadcasted_iota(jnp.int32, (total_rows, LANES), 0).astype(jnp.float32)
    doc_cols = dcol[...]
    row_doc = jnp.sum(jnp.where(place == row_pos, doc_cols, 0.0), axis=0, keepdims=True)
    row_first = jnp.sum(jnp.where(doc_cols < row_doc, 1.0, 0.0), axis=0, keepdims=True)
    first_rows = columns_of(row_first)
    pick = (sub == lane % step)[:step]

    def along(block):
        return jnp.sum(jnp.where(pick, block, 0.0), axis=0, keepdims=True)

    found = []
    for g in range(GROUPS):
        places = [slice(n * rows + g * step, n * rows + (g + 1) * step) for n in range(2)]
        found.append(
            tuple(
                jnp.concatenate([along(block[cut]) for cut in places], axis=1)
                for block in (own_rows, first_rows)
            )
        )

    def dot(a, b, ca, cb):
        return lax.dot_general(
            a, b, (((ca,), (cb,)), ((), ())), preferred_element_type=jnp.float32
        )

    def attend(g):
        pos, first = found[g]
        low, high = max(g - 1, 0) * step, (g + 1) * step
        span = high - low
        key_count = ctx_count * span
        cut = slice(g * step, (g + 1) * step)
        own_cut = pl.ds(pl.multiple_of(col * rows + g * step, step), step)
        key_block = kv[:, low:high, 0:head].reshape(key_count, head)
        value_block = kv[:, low:high, head : 2 * head].reshape(key_count, head)
        key_pos = kpos[:, low:high, :].reshape(key_count, LANES)
        key_pos = jnp.concatenate([key_pos, key_pos], axis=1)
        query_n = jnp.concatenate(
            [heads_of(q_ref[col, cut, :]), heads_of(q_in[cut, :])], axis=0
        )
        grad_n = jnp.concatenate(
            [heads_of(g_ref[col, cut, :]), heads_of(g_in[cut, :])], axis=0
        )
        delta = jnp.concatenate([delta_own[g : g + 1, :], delta_in[g : g + 1, :]], axis=1)
        live = (key_pos <= pos) & (key_pos >= first)
        scores = jnp.where(live, dot(key_block, query_n, 1, 1) * scale, NEG_FILL)
        terms = jnp.exp(scores - jnp.max(scores, axis=0, keepdims=True))
        probs = terms * (1.0 / jnp.sum(terms, axis=0, keepdims=True))
        prob_grad = dot(value_block, grad_n, 1, 1)
        score_grad = (probs * (prob_grad - delta)).astype(jnp.bfloat16)
        value_grad = dot(probs.astype(jnp.bfloat16), grad_n, 1, 0)
        key_grad = dot(score_grad, query_n, 1, 0) * scale
        query_grad = (dot(score_grad, key_block, 0, 0) * scale).astype(jnp.bfloat16)
        for h in range(heads):
            cols = slice(h * head, (h + 1) * head)
            dq_ref[own_cut, cols] = query_grad[h * step : (h + 1) * step]
            dq_out[cut, cols] = query_grad[(heads + h) * step : (heads + h + 1) * step]
        for part, grad in ((0, key_grad), (1, value_grad)):
            grad = grad.reshape(outer, 2, 2, span, head)
            cols = slice(part * head, (part + 1) * head)
            if span > step:
                acc[g - 1, :, :, :, :, cols] += grad[:, :, :, :step]
            acc[g, :, :, :, :, cols] = grad[:, :, :, span - step :]

    def y_start(b):
        y_out[b] = acc[b, :, (row + 1) % 2].astype(jnp.bfloat16)
        send(y_out.at[b], y_in.at[b], y_recv.at[b], across, pair)

    def z_start(b):
        landed(y_in.at[b], y_recv.at[b])
        y_sum[b] = acc[b, :, row] + y_in[b].astype(jnp.float32)
        for m in range(1, outer):
            z_out[b, m - 1] = y_sum[b, outer_of(m)].astype(jnp.bfloat16)
            send(
                z_out.at[b, m - 1],
                z_in.at[b, m - 1],
                z_recv.at[b, m - 1],
                ctx_of(outer_of(m), i_me),
                pair,
            )

    def z_finish(b):
        total = y_sum[b, o_me]
        for m in range(1, outer):
            landed(z_in.at[b, m - 1], z_recv.at[b, m - 1])
            total += z_in[b, m - 1].astype(jnp.float32)
        z_sum[:, b * step : (b + 1) * step, :] = total.astype(jnp.bfloat16)

    def wait_half(h):
        for o in range(outer):
            landed(*both_of(outer_of(o), (row + 1) % 2, h))

    def kvg_at(r, e, s):
        return kvg.at[e, pl.ds(2 * r, 2), s], kvg_recv.at[e, r, s]

    def pass_on(r, s):
        for e in range(1, pairs):
            dst, recv_sem = kvg_at(r, e, s)
            send(kvg_at(r, 0, s)[0], dst, recv_sem, me, (pair + e) % pairs)

    def kvg_start():
        for k in range(1, INNER):
            dst, recv_sem = kvg_at(k // 2, 0, col)
            send(z_sum, dst, recv_sem, ctx_of(o_me, inner_of(k)), pair)
        kvg[0, 0:2, col] = z_sum[...]
        pass_on(0, col)

    def kvg_forward(r, s):
        landed(*kvg_at(r, 0, s))
        pass_on(r, s)

    def x_turn(chosen):
        for n, (k, e) in enumerate(slots):
            if k == chosen:
                for o in range(x_parts):
                    if n:
                        landed(x_target(slot_of(k, e, col), o), x_recv.at[n - 1, o])
                    else:
                        own_copies[o].wait()
                slot = slot_of(k, e, col)
                cut = pl.ds(pl.multiple_of(slot * (seqs * rows), seqs * rows), seqs * rows)
                for o in range(outer):
                    xt[o, :, cut] = xg[slot, o].T

    x_start(3)
    x_start(1)
    wait_half(0)
    landed(delta_in, side_recv.at[0])
    for g in range(GROUPS):
        cut = pl.ds(g * step, step)
        landed(q_in.at[cut], swap_recv.at[g, 0])
        landed(g_in.at[cut], swap_recv.at[g, 1])
        if g == GROUPS // HALVES:
            wait_half(1)
            x_start(2, 0, (x_parts + 1) // 2)
        attend(g)
        if g >= 1:
            y_start(g - 1)
        if g >= 2:
            z_start(g - 2)
    y_start(GROUPS - 1)
    send(dq_out, dq_in, side_recv.at[1], side, pair)
    x_start(2, (x_parts + 1) // 2)
    z_start(GROUPS - 2)
    z_start(GROUPS - 1)
    x_turn(0)
    x_turn(1)
    for b in range(GROUPS):
        z_finish(b)
    kvg_start()
    x_turn(3)
    kvg_forward(0, other)
    kvg_forward(1, col)
    kvg_forward(1, other)
    x_turn(2)
    landed(dq_in, side_recv.at[1])
    dq_ref[pl.ds(pl.multiple_of(other * rows, rows), rows), :] = dq_in[...]
    for e in range(1, pairs):
        for r in range(2):
            for s in range(seqs):
                landed(*kvg_at(r, e, s))

    depth = len(slots) * seqs * rows
    kv_grads = kvg[...].reshape(depth, 2 * head)
    for m in range(1, outer):
        w_out[m - 1] = dot(xt[outer_of(m)], kv_grads, 1, 0).astype(jnp.bfloat16)
        send(
            w_out.at[m - 1], w_in.at[m - 1], w_recv.at[m - 1], ctx_of(outer_of(m), i_me), pair
        )
    wsum[...] = dot(xt[o_me], kv_grads, 1, 0)
    total = wsum[...]
    for m in range(1, outer):
        landed(w_in.at[m - 1], w_recv.at[m - 1])
        total += w_in[m - 1].astype(jnp.float32)
    w_fin[pair] = total[:width]
    for e in range(1, pairs):
        send(w_fin.at[pair], w_fin.at[pair], fin_recv.at[e - 1], me, (pair + e) % pairs)
    for e in range(1, pairs):
        landed(w_fin.at[(pair + pairs - e) % pairs], fin_recv.at[e - 1])
    dw_ref[...] = w_fin[...].reshape(dw_ref.shape)
    for copy in pending:
        copy.wait_send()


def local(
    layer_input, queries, key_states, value_states, attn_output, out_grad, doc_ids, positions
):
    seqs, rows, model = layer_input.shape
    head = key_states.shape[2]
    ctx = lax.axis_size("ctx")
    pairs = lax.axis_size("dp")
    outer = ctx // INNER
    width = model // (ctx * pairs)
    padded = -(-width // LANES) * LANES
    slots = INNER * pairs
    flat_rows = seqs * rows
    flat = layer_input.reshape(flat_rows, model)
    if padded == width:
        x_parts = outer
    else:
        x_parts = 1
        flat = flat.reshape(flat_rows, outer, INNER * pairs, width).transpose(2, 1, 0, 3)
        flat = jnp.pad(flat, ((0, 0), (0, 0), (0, 0), (0, padded - width)))
    vmem = pl.BlockSpec(memory_space=pltpu.VMEM)
    both = 2 * head
    sends = HALVES * 2 * outer + 2 * GROUPS + 2 + GROUPS * outer + 3 + 4 * (pairs - 1)
    sends += (slots - 1) * x_parts + (outer - 1) + (pairs - 1)
    dma = pltpu.SemaphoreType.DMA
    f32, bf16 = jnp.float32, jnp.bfloat16
    step = rows // GROUPS
    query_width = queries.shape[2]
    query_grad, weight_grad = pl.pallas_call(
        functools.partial(kernel, (outer, pairs, width)),
        out_shape=(
            jax.ShapeDtypeStruct((flat_rows, query_width), bf16),
            jax.ShapeDtypeStruct((model // ctx, both), f32),
        ),
        in_specs=[pl.BlockSpec(memory_space=pl.ANY)] + [vmem] * 7,
        out_specs=(vmem, vmem),
        scratch_shapes=[
            pltpu.VMEM((ctx, rows, both), bf16),
            pltpu.VMEM((rows, both), bf16),
            pltpu.VMEM((rows, query_width), bf16),
            pltpu.VMEM((rows, query_width), bf16),
            pltpu.VMEM((8, LANES), f32),
            pltpu.VMEM((8, LANES), f32),
            pltpu.VMEM((8, LANES), f32),
            pltpu.VMEM((rows, query_width), bf16),
            pltpu.VMEM((rows, query_width), bf16),
            pltpu.VMEM((ctx, rows, LANES), f32),
            pltpu.VMEM((ctx * rows, LANES), f32),
            pltpu.VMEM((GROUPS, outer, 2, 2, step, both), f32),
            pltpu.VMEM((GROUPS, outer, 2, step, both), bf16),
            pltpu.VMEM((GROUPS, outer, 2, step, both), bf16),
            pltpu.VMEM((GROUPS, outer, 2, step, both), f32),
            pltpu.VMEM((GROUPS, outer - 1, 2, step, both), bf16),
            pltpu.VMEM((GROUPS, outer - 1, 2, step, both), bf16),
            pltpu.VMEM((2, rows, both), bf16),
            pltpu.VMEM((pairs, INNER, seqs, rows, both), bf16),
            pltpu.VMEM((slots, outer, flat_rows, padded), bf16),
            pltpu.VMEM((outer, padded, slots * flat_rows), bf16),
            pltpu.VMEM((padded, both), f32),
            pltpu.VMEM((outer - 1, padded, both), bf16),
            pltpu.VMEM((outer - 1, padded, both), bf16),
            pltpu.VMEM((pairs, width, both), f32),
            dma((sends,)),
            dma((GROUPS, 2)),
            dma((2,)),
            dma((HALVES,)),
            dma((HALVES, 2 * outer)),
            dma((GROUPS,)),
            dma((GROUPS, outer - 1)),
            dma((pairs, 2, seqs)),
            dma((slots - 1, x_parts)),
            dma((outer - 1,)),
            dma((pairs - 1,)),
            dma((x_parts,)),
        ],
        compiler_params=pltpu.CompilerParams(
            collective_id=0, has_side_effects=True, vmem_limit_bytes=60 * 1024 * 1024
        ),
    )(flat, queries, key_states, value_states, attn_output, out_grad, doc_ids, positions)
    return query_grad.reshape(queries.shape), weight_grad


def solution(mesh):
    in_specs = (
        P("dp", "ctx", None),
        P("dp", "ctx", None),
        P("dp", "ctx", None),
        P("dp", "ctx", None),
        P("dp", "ctx", None),
        P("dp", "ctx", None),
        P("dp", None),
        P("dp", None),
    )
    out_specs = (P("dp", "ctx", None), P("ctx", None))
    return jax.shard_map(local, mesh=mesh, in_specs=in_specs, out_specs=out_specs, check_vma=False)
```

```python
import functools
import math

import jax
import jax.numpy as jnp
from jax import lax
from jax.experimental import pallas as pl
from jax.experimental.pallas import tpu as pltpu
from jax.sharding import PartitionSpec as P

NEG_FILL = -1e30
INNER = 4
LANES = 128


GROUPS = 4
HALVES = 2


def kernel(
    dims,
    x_ref,
    q_ref,
    k_ref,
    v_ref,
    a_ref,
    g_ref,
    doc_ref,
    pos_ref,
    dq_ref,
    dw_ref,
    kv,
    kv_swap,
    q_in,
    g_in,
    delta_own,
    delta_out,
    delta_in,
    dq_out,
    dq_in,
    kpos,
    dcol,
    acc,
    y_out,
    y_in,
    y_sum,
    z_out,
    z_in,
    z_sum,
    kvg,
    xg,
    xt,
    wsum,
    wy_out,
    wy_in,
    w_out,
    w_in,
    w_fin,
    send_sem,
    swap_recv,
    side_recv,
    ag_recv,
    y_recv,
    z_recv,
    kvg_recv,
    x_recv,
    wy_recv,
    w_recv,
    fin_recv,
    own_sem,
):
    outer, pairs, width = dims
    seqs, rows, head = k_ref.shape
    heads = q_ref.shape[2] // head
    step = rows // GROUPS
    scale = 1.0 / math.sqrt(head)
    x_parts = 2 * outer if x_ref.ndim == 2 else 1
    ctx_count = outer * INNER

    me = lax.axis_index("ctx")
    pair = lax.axis_index("dp")
    o_me, i_me = me // INNER, me % INNER
    col, row = i_me % 2, i_me // 2
    other = (col + 1) % 2

    def inner_of(k):
        return ((row + k // 2) % 2) * 2 + (col + k % 2) % 2

    def outer_of(m):
        return (o_me + m) % outer

    def ctx_of(o, i):
        return o * INNER + i

    side, across = ctx_of(o_me, inner_of(1)), ctx_of(o_me, inner_of(2))

    pending = []

    def copy_to(src, dst, recv_sem, ctx, dp, slot):
        return pltpu.make_async_remote_copy(
            src_ref=src,
            dst_ref=dst,
            send_sem=send_sem.at[slot],
            recv_sem=recv_sem,
            device_id={"ctx": ctx, "dp": dp},
            device_id_type=pl.DeviceIdType.MESH,
        )

    def send(src, dst, recv_sem, ctx, dp):
        copy = copy_to(src, dst, recv_sem, ctx, dp, len(pending))
        copy.start()
        pending.append(copy)

    def landed(dst, recv_sem):
        copy_to(dst, dst, recv_sem, side, pair, 0).wait_recv()

    slots = [(k, e) for k in range(2) for e in range(pairs)]

    barrier = pltpu.get_barrier_semaphore()
    greeted = [(ctx_of(outer_of(m), i_me), pair) for m in range(1, outer)]
    greeted += [(across, pair)]
    greeted += [(ctx_of(o_me, inner_of(k)), (pair + e) % pairs) for k, e in slots[1:]]
    for ctx, dp in greeted:
        pl.semaphore_signal(
            barrier,
            inc=1,
            device_id={"ctx": ctx, "dp": dp},
            device_id_type=pl.DeviceIdType.MESH,
        )

    def heads_of(block):
        return jnp.concatenate(
            [block[:, h * head : (h + 1) * head] for h in range(heads)], axis=0
        )

    def delta_rows(s, g):
        cut = slice(g * step, (g + 1) * step)
        product = heads_of(g_ref[s, cut, :].astype(jnp.float32)) * heads_of(
            a_ref[s, cut, :].astype(jnp.float32)
        )
        return jnp.sum(product.T, axis=0, keepdims=True)

    kv[me, :, 0:head] = k_ref[col]
    kv[me, :, head : 2 * head] = v_ref[col]
    kv_swap[:, 0:head] = k_ref[other]
    kv_swap[:, head : 2 * head] = v_ref[other]
    pl.semaphore_wait(barrier, len(greeted))

    def half(h):
        return pl.ds(h * (rows // HALVES), rows // HALVES)

    def block_send(src, h, ctx):
        send(kv.at[src, half(h)], kv.at[src, half(h)], ag_recv.at[h, src], ctx, pair)

    def block_landed(src, h):
        landed(kv.at[src, half(h)], ag_recv.at[h, src])

    for h in range(HALVES):
        send(kv_swap.at[half(h)], kv.at[me, half(h)], ag_recv.at[h, me], side, pair)
        for m in range(1, outer):
            block_send(me, h, ctx_of(outer_of(m), i_me))
        block_send(me, h, across)
    for g in range(GROUPS):
        cut = pl.ds(g * step, step)
        send(q_ref.at[other, cut], q_in.at[cut], swap_recv.at[g, 0], side, pair)
        send(g_ref.at[other, cut], g_in.at[cut], swap_recv.at[g, 1], side, pair)
    def x_source(o, i, d):
        if x_ref.ndim == 2:
            first = ((o * 2 + i) * pairs + d) * width
            return x_ref.at[:, pl.ds(pl.multiple_of(first, LANES), width)]
        return x_ref.at[i * pairs + d]

    def slot_of(k, e, column):
        return e * 2 + (column + k) % 2

    def x_target(n, o):
        return xg.at[n, o] if x_ref.ndim == 2 else xg.at[n]

    own_copies = []
    for o in range(x_parts):
        own_copies.append(
            pltpu.make_async_copy(x_source(o, col, pair), x_target(slot_of(0, 0, col), o), own_sem.at[o])
        )
        own_copies[-1].start()

    def x_start(chosen):
        for n, (k, e) in enumerate(slots):
            if n and k == chosen:
                for o in range(x_parts):
                    send(
                        x_source(o, (col + k) % 2, (pair + e) % pairs),
                        x_target(slot_of(0, e, col), o),
                        x_recv.at[n - 1, o],
                        ctx_of(o_me, inner_of(k)),
                        (pair + e) % pairs,
                    )

    x_start(0)
    for h in range(HALVES):
        block_landed(side, h)
        for m in range(1, outer):
            block_send(side, h, ctx_of(outer_of(m), i_me))
        block_send(side, h, across)

    for g in range(GROUPS):
        delta_out[g : g + 1, :] = delta_rows(other, g)
    send(delta_out, delta_in, side_recv.at[0], side, pair)
    def forward(h):
        for m in range(1, outer):
            o = outer_of(outer - m)
            for src in (ctx_of(o, i_me), ctx_of(o, inner_of(1))):
                block_landed(src, h)
                block_send(src, h, across)

    forward(0)
    for g in range(GROUPS):
        delta_own[g : g + 1, :] = delta_rows(col, g)

    def columns_of(line):
        return jnp.broadcast_to(line, (LANES, LANES)).T

    total_rows = ctx_count * rows
    per = LANES // rows
    pos_line = pos_ref[pl.ds(col, 1), :].astype(jnp.float32)
    doc_line = doc_ref[pl.ds(col, 1), :].astype(jnp.float32)
    for b in range(total_rows // LANES):
        cut = slice(b * LANES, (b + 1) * LANES)
        kpos[b * per : (b + 1) * per] = columns_of(pos_line[:, cut]).reshape(per, rows, LANES)
        dcol[cut] = columns_of(doc_line[:, cut])

    forward(1)
    own_rows = jnp.concatenate([kpos[me], kpos[side]], axis=0)
    sub = lax.broadcasted_iota(jnp.int32, own_rows.shape, 0)
    lane = lax.broadcasted_iota(jnp.int32, own_rows.shape, 1)
    row_pos = jnp.sum(jnp.where(sub == lane, own_rows, 0.0), axis=0, keepdims=True)
    place = lax.broadcasted_iota(jnp.int32, (total_rows, LANES), 0).astype(jnp.float32)
    doc_cols = dcol[...]
    row_doc = jnp.sum(jnp.where(place == row_pos, doc_cols, 0.0), axis=0, keepdims=True)
    row_first = jnp.sum(jnp.where(doc_cols < row_doc, 1.0, 0.0), axis=0, keepdims=True)
    first_rows = columns_of(row_first)
    pick = (sub == lane % step)[:step]

    def along(block):
        return jnp.sum(jnp.where(pick, block, 0.0), axis=0, keepdims=True)

    found = []
    for g in range(GROUPS):
        places = [slice(n * rows + g * step, n * rows + (g + 1) * step) for n in range(2)]
        found.append(
            tuple(
                jnp.concatenate([along(block[cut]) for cut in places], axis=1)
                for block in (own_rows, first_rows)
            )
        )

    def dot(a, b, ca, cb):
        return lax.dot_general(
            a, b, (((ca,), (cb,)), ((), ())), preferred_element_type=jnp.float32
        )

    def attend(g):
        pos, first = found[g]
        low, high = max(g - 1, 0) * step, (g + 1) * step
        span = high - low
        key_count = ctx_count * span
        cut = slice(g * step, (g + 1) * step)
        own_cut = pl.ds(pl.multiple_of(col * rows + g * step, step), step)
        key_block = kv[:, low:high, 0:head].reshape(key_count, head)
        value_block = kv[:, low:high, head : 2 * head].reshape(key_count, head)
        key_pos = kpos[:, low:high, :].reshape(key_count, LANES)
        key_pos = jnp.concatenate([key_pos, key_pos], axis=1)
        query_n = jnp.concatenate(
            [heads_of(q_ref[col, cut, :]), heads_of(q_in[cut, :])], axis=0
        )
        grad_n = jnp.concatenate(
            [heads_of(g_ref[col, cut, :]), heads_of(g_in[cut, :])], axis=0
        )
        delta = jnp.concatenate([delta_own[g : g + 1, :], delta_in[g : g + 1, :]], axis=1)
        live = (key_pos <= pos) & (key_pos >= first)
        scores = jnp.where(live, dot(key_block, query_n, 1, 1) * scale, NEG_FILL)
        terms = jnp.exp(scores - jnp.max(scores, axis=0, keepdims=True))
        probs = terms * (1.0 / jnp.sum(terms, axis=0, keepdims=True))
        prob_grad = dot(value_block, grad_n, 1, 1)
        score_grad = (probs * (prob_grad - delta)).astype(jnp.bfloat16)
        value_grad = dot(probs.astype(jnp.bfloat16), grad_n, 1, 0)
        key_grad = dot(score_grad, query_n, 1, 0) * scale
        query_grad = (dot(score_grad, key_block, 0, 0) * scale).astype(jnp.bfloat16)
        for h in range(heads):
            cols = slice(h * head, (h + 1) * head)
            dq_ref[own_cut, cols] = query_grad[h * step : (h + 1) * step]
            dq_out[cut, cols] = query_grad[(heads + h) * step : (heads + h + 1) * step]
        for part, grad in ((0, key_grad), (1, value_grad)):
            grad = grad.reshape(outer, 2, 2, span, head)
            cols = slice(part * head, (part + 1) * head)
            if span > step:
                acc[g - 1, :, :, :, :, cols] += grad[:, :, :, :step]
            acc[g, :, :, :, :, cols] = grad[:, :, :, span - step :]

    def y_start(b):
        y_out[b] = acc[b, :, (row + 1) % 2].astype(jnp.bfloat16)
        send(y_out.at[b], y_in.at[b], y_recv.at[b], across, pair)

    def z_start(b):
        landed(y_in.at[b], y_recv.at[b])
        y_sum[b] = acc[b, :, row] + y_in[b].astype(jnp.float32)
        for m in range(1, outer):
            z_out[b, m - 1] = y_sum[b, outer_of(m)].astype(jnp.bfloat16)
            send(
                z_out.at[b, m - 1],
                z_in.at[b, m - 1],
                z_recv.at[b, m - 1],
                ctx_of(outer_of(m), i_me),
                pair,
            )

    def z_finish(b):
        total = y_sum[b, o_me]
        for m in range(1, outer):
            landed(z_in.at[b, m - 1], z_recv.at[b, m - 1])
            total += z_in[b, m - 1].astype(jnp.float32)
        z_sum[:, b * step : (b + 1) * step, :] = total.astype(jnp.bfloat16)

    def wait_half(h):
        for o in range(outer):
            for k in (2, 3):
                block_landed(ctx_of(outer_of(o), inner_of(k)), h)

    def kvg_at(e, s):
        return kvg.at[e, :, s], kvg_recv.at[e, s]

    def pass_on(s):
        for e in range(1, pairs):
            dst, recv_sem = kvg_at(e, s)
            send(kvg_at(0, s)[0], dst, recv_sem, me, (pair + e) % pairs)

    def x_turn(chosen):
        for n, (k, e) in enumerate(slots):
            if k == chosen:
                for o in range(x_parts):
                    if n:
                        landed(x_target(slot_of(k, e, col), o), x_recv.at[n - 1, o])
                    else:
                        own_copies[o].wait()
                slot = slot_of(k, e, col)
                cut = pl.ds(pl.multiple_of(slot * (seqs * rows), seqs * rows), seqs * rows)
                for o in range(2 * outer):
                    xt[o, :, cut] = xg[slot, o].T

    wait_half(0)
    landed(delta_in, side_recv.at[0])
    for g in range(GROUPS):
        cut = pl.ds(g * step, step)
        landed(q_in.at[cut], swap_recv.at[g, 0])
        landed(g_in.at[cut], swap_recv.at[g, 1])
        if g == GROUPS // HALVES:
            wait_half(1)
        attend(g)
        if g == 0:
            x_start(1)
        if g >= 1:
            y_start(g - 1)
        if g >= 2:
            z_start(g - 2)
    y_start(GROUPS - 1)
    send(dq_out, dq_in, side_recv.at[1], side, pair)
    z_start(GROUPS - 2)
    z_start(GROUPS - 1)
    x_turn(0)
    for b in range(GROUPS):
        z_finish(b)
    dst, recv_sem = kvg_at(0, col)
    send(z_sum, dst, recv_sem, side, pair)
    kvg[0, :, col] = z_sum[...]
    pass_on(col)
    x_turn(1)
    landed(*kvg_at(0, other))
    pass_on(other)
    landed(dq_in, side_recv.at[1])
    dq_ref[pl.ds(pl.multiple_of(other * rows, rows), rows), :] = dq_in[...]
    for e in range(1, pairs):
        for s in range(seqs):
            landed(*kvg_at(e, s))

    depth = len(slots) * seqs * rows
    kv_grads = kvg[...].reshape(depth, 2 * head)
    for n in range(outer):
        o = outer_of((n + 1) % outer)
        wy_out[n] = dot(xt[o * 2 + (row + 1) % 2], kv_grads, 1, 0).astype(jnp.bfloat16)
        send(wy_out.at[n], wy_in.at[n], wy_recv.at[n], across, pair)
    for n in range(outer):
        wsum[n] = dot(xt[outer_of((n + 1) % outer) * 2 + row], kv_grads, 1, 0)
    for n in range(outer):
        landed(wy_in.at[n], wy_recv.at[n])
        total = wsum[n] + wy_in[n].astype(jnp.float32)
        if n < outer - 1:
            w_out[n] = total.astype(jnp.bfloat16)
            send(w_out.at[n], w_in.at[n], w_recv.at[n], ctx_of(outer_of(n + 1), i_me), pair)
    for m in range(1, outer):
        landed(w_in.at[m - 1], w_recv.at[m - 1])
        total += w_in[m - 1].astype(jnp.float32)
    w_fin[pair] = total[:width]
    for e in range(1, pairs):
        send(w_fin.at[pair], w_fin.at[pair], fin_recv.at[e - 1], me, (pair + e) % pairs)
    for e in range(1, pairs):
        landed(w_fin.at[(pair + pairs - e) % pairs], fin_recv.at[e - 1])
    dw_ref[...] = w_fin[...].reshape(dw_ref.shape)
    for copy in pending:
        copy.wait_send()


def local(
    layer_input, queries, key_states, value_states, attn_output, out_grad, doc_ids, positions
):
    seqs, rows, model = layer_input.shape
    head = key_states.shape[2]
    ctx = lax.axis_size("ctx")
    pairs = lax.axis_size("dp")
    outer = ctx // INNER
    width = model // (ctx * pairs)
    padded = -(-width // LANES) * LANES
    slots = 2 * pairs
    flat_rows = seqs * rows
    flat = layer_input.reshape(flat_rows, model)
    if padded == width:
        x_parts = 2 * outer
    else:
        x_parts = 1
        flat = flat.reshape(flat_rows, 2 * outer, 2 * pairs, width).transpose(2, 1, 0, 3)
        flat = jnp.pad(flat, ((0, 0), (0, 0), (0, 0), (0, padded - width)))
    vmem = pl.BlockSpec(memory_space=pltpu.VMEM)
    both = 2 * head
    sends = HALVES * (4 * outer + 1) + 2 * GROUPS + 2 + GROUPS * outer + 1 + 2 * (pairs - 1)
    sends += (slots - 1) * x_parts + outer + (outer - 1) + (pairs - 1)
    dma = pltpu.SemaphoreType.DMA
    f32, bf16 = jnp.float32, jnp.bfloat16
    step = rows // GROUPS
    query_width = queries.shape[2]
    query_grad, weight_grad = pl.pallas_call(
        functools.partial(kernel, (outer, pairs, width)),
        out_shape=(
            jax.ShapeDtypeStruct((flat_rows, query_width), bf16),
            jax.ShapeDtypeStruct((model // ctx, both), f32),
        ),
        in_specs=[pl.BlockSpec(memory_space=pl.ANY)] + [vmem] * 7,
        out_specs=(vmem, vmem),
        scratch_shapes=[
            pltpu.VMEM((ctx, rows, both), bf16),
            pltpu.VMEM((rows, both), bf16),
            pltpu.VMEM((rows, query_width), bf16),
            pltpu.VMEM((rows, query_width), bf16),
            pltpu.VMEM((8, LANES), f32),
            pltpu.VMEM((8, LANES), f32),
            pltpu.VMEM((8, LANES), f32),
            pltpu.VMEM((rows, query_width), bf16),
            pltpu.VMEM((rows, query_width), bf16),
            pltpu.VMEM((ctx, rows, LANES), f32),
            pltpu.VMEM((ctx * rows, LANES), f32),
            pltpu.VMEM((GROUPS, outer, 2, 2, step, both), f32),
            pltpu.VMEM((GROUPS, outer, 2, step, both), bf16),
            pltpu.VMEM((GROUPS, outer, 2, step, both), bf16),
            pltpu.VMEM((GROUPS, outer, 2, step, both), f32),
            pltpu.VMEM((GROUPS, outer - 1, 2, step, both), bf16),
            pltpu.VMEM((GROUPS, outer - 1, 2, step, both), bf16),
            pltpu.VMEM((2, rows, both), bf16),
            pltpu.VMEM((pairs, 2, seqs, rows, both), bf16),
            pltpu.VMEM((slots, 2 * outer, flat_rows, padded), bf16),
            pltpu.VMEM((2 * outer, padded, slots * flat_rows), bf16),
            pltpu.VMEM((outer, padded, both), f32),
            pltpu.VMEM((outer, padded, both), bf16),
            pltpu.VMEM((outer, padded, both), bf16),
            pltpu.VMEM((outer - 1, padded, both), bf16),
            pltpu.VMEM((outer - 1, padded, both), bf16),
            pltpu.VMEM((pairs, width, both), f32),
            dma((sends,)),
            dma((GROUPS, 2)),
            dma((2,)),
            dma((HALVES, ctx)),
            dma((GROUPS,)),
            dma((GROUPS, outer - 1)),
            dma((pairs, seqs)),
            dma((slots - 1, x_parts)),
            dma((outer,)),
            dma((outer - 1,)),
            dma((pairs - 1,)),
            dma((x_parts,)),
        ],
        compiler_params=pltpu.CompilerParams(
            collective_id=0, has_side_effects=True, vmem_limit_bytes=60 * 1024 * 1024
        ),
    )(flat, queries, key_states, value_states, attn_output, out_grad, doc_ids, positions)
    return query_grad.reshape(queries.shape), weight_grad


def solution(mesh):
    in_specs = (
        P("dp", "ctx", None),
        P("dp", "ctx", None),
        P("dp", "ctx", None),
        P("dp", "ctx", None),
        P("dp", "ctx", None),
        P("dp", "ctx", None),
        P("dp", None),
        P("dp", None),
    )
    out_specs = (P("dp", "ctx", None), P("ctx", None))
    return jax.shard_map(local, mesh=mesh, in_specs=in_specs, out_specs=out_specs, check_vma=False)
```

```python
import functools
import math

import jax
import jax.numpy as jnp
from jax import lax
from jax.experimental import pallas as pl
from jax.experimental.pallas import tpu as pltpu
from jax.sharding import PartitionSpec as P

NEG_FILL = -1e30
INNER = 4
LANES = 128


GROUPS = 4
HALVES = 2


def kernel(
    dims,
    x_ref,
    q_ref,
    k_ref,
    v_ref,
    a_ref,
    g_ref,
    doc_ref,
    pos_ref,
    dq_ref,
    dw_ref,
    kv,
    kv_swap,
    q_in,
    g_in,
    delta_own,
    delta_out,
    delta_in,
    dq_out,
    dq_in,
    kpos,
    dcol,
    acc,
    y_out,
    y_in,
    y_sum,
    z_out,
    z_in,
    z_sum,
    kvg,
    xg,
    xt,
    wsum,
    wy_out,
    wy_in,
    w_out,
    w_in,
    w_fin,
    send_sem,
    swap_recv,
    side_recv,
    ag_recv,
    y_recv,
    z_recv,
    kvg_recv,
    x_recv,
    wy_recv,
    w_recv,
    fin_recv,
    own_sem,
):
    outer, pairs, width = dims
    seqs, rows, head = k_ref.shape
    heads = q_ref.shape[2] // head
    step = rows // GROUPS
    scale = 1.0 / math.sqrt(head)
    x_parts = 2 * outer if x_ref.ndim == 2 else 1
    ctx_count = outer * INNER

    me = lax.axis_index("ctx")
    pair = lax.axis_index("dp")
    o_me, i_me = me // INNER, me % INNER
    col, row = i_me % 2, i_me // 2
    other = (col + 1) % 2

    def inner_of(k):
        return ((row + k // 2) % 2) * 2 + (col + k % 2) % 2

    def outer_of(m):
        return (o_me + m) % outer

    def ctx_of(o, i):
        return o * INNER + i

    side, across = ctx_of(o_me, inner_of(1)), ctx_of(o_me, inner_of(2))

    pending = []

    def copy_to(src, dst, recv_sem, ctx, dp, slot):
        return pltpu.make_async_remote_copy(
            src_ref=src,
            dst_ref=dst,
            send_sem=send_sem.at[slot],
            recv_sem=recv_sem,
            device_id={"ctx": ctx, "dp": dp},
            device_id_type=pl.DeviceIdType.MESH,
        )

    def send(src, dst, recv_sem, ctx, dp):
        copy = copy_to(src, dst, recv_sem, ctx, dp, len(pending))
        copy.start()
        pending.append(copy)

    def landed(dst, recv_sem):
        copy_to(dst, dst, recv_sem, side, pair, 0).wait_recv()

    slots = [(k, e) for k in range(2) for e in range(pairs)]

    barrier = pltpu.get_barrier_semaphore()
    greeted = [(ctx_of(outer_of(m), i_me), pair) for m in range(1, outer)]
    greeted += [(across, pair)]
    greeted += [(ctx_of(o_me, inner_of(k)), (pair + e) % pairs) for k, e in slots[1:]]
    for ctx, dp in greeted:
        pl.semaphore_signal(
            barrier,
            inc=1,
            device_id={"ctx": ctx, "dp": dp},
            device_id_type=pl.DeviceIdType.MESH,
        )

    def heads_of(block):
        return jnp.concatenate(
            [block[:, h * head : (h + 1) * head] for h in range(heads)], axis=0
        )

    def delta_rows(s, g):
        cut = slice(g * step, (g + 1) * step)
        product = heads_of(g_ref[s, cut, :].astype(jnp.float32)) * heads_of(
            a_ref[s, cut, :].astype(jnp.float32)
        )
        return jnp.sum(product.T, axis=0, keepdims=True)

    kv[me, :, 0:head] = k_ref[col]
    kv[me, :, head : 2 * head] = v_ref[col]
    kv_swap[:, 0:head] = k_ref[other]
    kv_swap[:, head : 2 * head] = v_ref[other]
    pl.semaphore_wait(barrier, len(greeted))

    def half(h):
        return pl.ds(h * (rows // HALVES), rows // HALVES)

    def block_send(src, h, ctx):
        send(kv.at[src, half(h)], kv.at[src, half(h)], ag_recv.at[h, src], ctx, pair)

    def block_landed(src, h):
        landed(kv.at[src, half(h)], ag_recv.at[h, src])

    for h in range(HALVES):
        send(kv_swap.at[half(h)], kv.at[me, half(h)], ag_recv.at[h, me], side, pair)
        for m in range(1, outer):
            block_send(me, h, ctx_of(outer_of(m), i_me))
        block_send(me, h, across)
    for g in range(GROUPS):
        cut = pl.ds(g * step, step)
        send(q_ref.at[other, cut], q_in.at[cut], swap_recv.at[g, 0], side, pair)
        send(g_ref.at[other, cut], g_in.at[cut], swap_recv.at[g, 1], side, pair)
    def x_source(o, i, d):
        if x_ref.ndim == 2:
            first = ((o * 2 + i) * pairs + d) * width
            return x_ref.at[:, pl.ds(pl.multiple_of(first, LANES), width)]
        return x_ref.at[i * pairs + d]

    def slot_of(k, e, column):
        return e * 2 + (column + k) % 2

    def x_target(n, o):
        return xg.at[n, o] if x_ref.ndim == 2 else xg.at[n]

    def slot_of(k, e, column):
        return e * 2 + (column + k) % 2

    def x_target(n, o):
        return xg.at[n, o] if x_ref.ndim == 2 else xg.at[n]

    own_copies = []
    for o in range(x_parts):
        own_copies.append(
            pltpu.make_async_copy(x_source(o, col, pair), x_target(slot_of(0, 0, col), o), own_sem.at[o])
        )
        own_copies[-1].start()

    def x_start(chosen):
        for n, (k, e) in enumerate(slots):
            if n and k == chosen:
                for o in range(x_parts):
                    send(
                        x_source(o, (col + k) % 2, (pair + e) % pairs),
                        x_target(slot_of(0, e, col), o),
                        x_recv.at[n - 1, o],
                        ctx_of(o_me, inner_of(k)),
                        (pair + e) % pairs,
                    )

    for h in range(HALVES):
        block_landed(side, h)
        for m in range(1, outer):
            block_send(side, h, ctx_of(outer_of(m), i_me))
        block_send(side, h, across)

    for g in range(GROUPS):
        delta_out[g : g + 1, :] = delta_rows(other, g)
    send(delta_out, delta_in, side_recv.at[0], side, pair)
    def forward(h):
        for m in range(1, outer):
            o = outer_of(outer - m)
            for src in (ctx_of(o, i_me), ctx_of(o, inner_of(1))):
                block_landed(src, h)
                block_send(src, h, across)

    forward(0)
    for g in range(GROUPS):
        delta_own[g : g + 1, :] = delta_rows(col, g)

    def columns_of(line):
        return jnp.broadcast_to(line, (LANES, LANES)).T

    total_rows = ctx_count * rows
    per = LANES // rows
    pos_line = pos_ref[pl.ds(col, 1), :].astype(jnp.float32)
    doc_line = doc_ref[pl.ds(col, 1), :].astype(jnp.float32)
    for b in range(total_rows // LANES):
        cut = slice(b * LANES, (b + 1) * LANES)
        kpos[b * per : (b + 1) * per] = columns_of(pos_line[:, cut]).reshape(per, rows, LANES)
        dcol[cut] = columns_of(doc_line[:, cut])

    forward(1)
    x_start(0)

    own_rows = jnp.concatenate([kpos[me], kpos[side]], axis=0)
    sub = lax.broadcasted_iota(jnp.int32, own_rows.shape, 0)
    lane = lax.broadcasted_iota(jnp.int32, own_rows.shape, 1)
    row_pos = jnp.sum(jnp.where(sub == lane, own_rows, 0.0), axis=0, keepdims=True)
    place = lax.broadcasted_iota(jnp.int32, (total_rows, LANES), 0).astype(jnp.float32)
    doc_cols = dcol[...]
    row_doc = jnp.sum(jnp.where(place == row_pos, doc_cols, 0.0), axis=0, keepdims=True)
    row_first = jnp.sum(jnp.where(doc_cols < row_doc, 1.0, 0.0), axis=0, keepdims=True)
    first_rows = columns_of(row_first)
    pick = (sub == lane % step)[:step]

    def along(block):
        return jnp.sum(jnp.where(pick, block, 0.0), axis=0, keepdims=True)

    found = []
    for g in range(GROUPS):
        places = [slice(n * rows + g * step, n * rows + (g + 1) * step) for n in range(2)]
        found.append(
            tuple(
                jnp.concatenate([along(block[cut]) for cut in places], axis=1)
                for block in (own_rows, first_rows)
            )
        )

    def dot(a, b, ca, cb):
        return lax.dot_general(
            a, b, (((ca,), (cb,)), ((), ())), preferred_element_type=jnp.float32
        )

    def attend(g):
        pos, first = found[g]
        low, high = max(g - 1, 0) * step, (g + 1) * step
        span = high - low
        key_count = ctx_count * span
        cut = slice(g * step, (g + 1) * step)
        own_cut = pl.ds(pl.multiple_of(col * rows + g * step, step), step)
        key_block = kv[:, low:high, 0:head].reshape(key_count, head)
        value_block = kv[:, low:high, head : 2 * head].reshape(key_count, head)
        key_pos = kpos[:, low:high, :].reshape(key_count, LANES)
        key_pos = jnp.concatenate([key_pos, key_pos], axis=1)
        query_n = jnp.concatenate(
            [heads_of(q_ref[col, cut, :]), heads_of(q_in[cut, :])], axis=0
        )
        grad_n = jnp.concatenate(
            [heads_of(g_ref[col, cut, :]), heads_of(g_in[cut, :])], axis=0
        )
        delta = jnp.concatenate([delta_own[g : g + 1, :], delta_in[g : g + 1, :]], axis=1)
        live = (key_pos <= pos) & (key_pos >= first)
        scores = jnp.where(live, dot(key_block, query_n, 1, 1), NEG_FILL)
        drop = scores - jnp.max(scores, axis=0, keepdims=True)
        terms = jnp.exp2(drop * (scale * math.log2(math.e)))
        probs = terms * (1.0 / jnp.sum(terms, axis=0, keepdims=True))
        prob_grad = dot(value_block, grad_n, 1, 1)
        score_grad = (probs * (prob_grad - delta)).astype(jnp.bfloat16)
        value_grad = dot(probs.astype(jnp.bfloat16), grad_n, 1, 0)
        key_grad = dot(score_grad, query_n, 1, 0) * scale
        query_grad = (dot(score_grad, key_block, 0, 0) * scale).astype(jnp.bfloat16)
        for h in range(heads):
            cols = slice(h * head, (h + 1) * head)
            dq_ref[own_cut, cols] = query_grad[h * step : (h + 1) * step]
            dq_out[cut, cols] = query_grad[(heads + h) * step : (heads + h + 1) * step]
        for part, grad in ((0, key_grad), (1, value_grad)):
            grad = grad.reshape(outer, 2, 2, span, head)
            cols = slice(part * head, (part + 1) * head)
            if span > step:
                acc[g - 1, :, :, :, :, cols] += grad[:, :, :, :step]
            acc[g, :, :, :, :, cols] = grad[:, :, :, span - step :]

    def y_start(b):
        y_out[b] = acc[b, :, (row + 1) % 2].astype(jnp.bfloat16)
        send(y_out.at[b], y_in.at[b], y_recv.at[b], across, pair)

    def z_start(b):
        landed(y_in.at[b], y_recv.at[b])
        y_sum[b] = acc[b, :, row] + y_in[b].astype(jnp.float32)
        for m in range(1, outer):
            z_out[b, m - 1] = y_sum[b, outer_of(m)].astype(jnp.bfloat16)
            send(
                z_out.at[b, m - 1],
                z_in.at[b, m - 1],
                z_recv.at[b, m - 1],
                ctx_of(outer_of(m), i_me),
                pair,
            )

    def z_finish(b):
        total = y_sum[b, o_me]
        for m in range(1, outer):
            landed(z_in.at[b, m - 1], z_recv.at[b, m - 1])
            total += z_in[b, m - 1].astype(jnp.float32)
        z_sum[:, b * step : (b + 1) * step, :] = total.astype(jnp.bfloat16)

    def wait_half(h):
        for o in range(outer):
            for k in (2, 3):
                block_landed(ctx_of(outer_of(o), inner_of(k)), h)

    def kvg_at(e, s, h):
        return kvg.at[e, :, s, half(h)], kvg_recv.at[e, s, h]

    def pass_on(s, h):
        for e in range(1, pairs):
            dst, recv_sem = kvg_at(e, s, h)
            send(kvg_at(0, s, h)[0], dst, recv_sem, me, (pair + e) % pairs)

    def x_turn(chosen):
        for n, (k, e) in enumerate(slots):
            if k == chosen:
                for o in range(x_parts):
                    if n:
                        landed(x_target(slot_of(k, e, col), o), x_recv.at[n - 1, o])
                    else:
                        own_copies[o].wait()
                slot = slot_of(k, e, col)
                cut = pl.ds(pl.multiple_of(slot * (seqs * rows), seqs * rows), seqs * rows)
                for o in range(2 * outer):
                    xt[o, :, cut] = xg[slot, o].T

    wait_half(0)
    landed(delta_in, side_recv.at[0])
    for g in range(GROUPS):
        cut = pl.ds(g * step, step)
        landed(q_in.at[cut], swap_recv.at[g, 0])
        landed(g_in.at[cut], swap_recv.at[g, 1])
        if g == GROUPS // HALVES:
            wait_half(1)
        if g == 0:
            x_start(1)
        attend(g)
        if g >= 1:
            y_start(g - 1)
        if g >= 2:
            z_start(g - 2)
    y_start(GROUPS - 1)
    z_start(GROUPS - 2)
    z_start(GROUPS - 1)
    x_turn(0)
    for h in range(HALVES):
        for b in range(h * GROUPS // HALVES, (h + 1) * GROUPS // HALVES):
            z_finish(b)
        dst, recv_sem = kvg_at(0, col, h)
        send(z_sum.at[:, half(h)], dst, recv_sem, side, pair)
        kvg[0, :, col, half(h)] = z_sum[:, half(h)]
        pass_on(col, h)
    send(dq_out, dq_in, side_recv.at[1], side, pair)
    x_turn(1)
    for h in range(HALVES):
        landed(*kvg_at(0, other, h))
        pass_on(other, h)
    landed(dq_in, side_recv.at[1])
    dq_ref[pl.ds(pl.multiple_of(other * rows, rows), rows), :] = dq_in[...]
    for e in range(1, pairs):
        for s in range(seqs):
            for h in range(HALVES):
                landed(*kvg_at(e, s, h))

    depth = len(slots) * seqs * rows
    kv_grads = kvg[...].reshape(depth, 2 * head)
    for n in range(outer):
        o = outer_of((n + 1) % outer)
        wy_out[n] = dot(xt[o * 2 + (row + 1) % 2], kv_grads, 1, 0).astype(jnp.bfloat16)
        send(wy_out.at[n], wy_in.at[n], wy_recv.at[n], across, pair)
    for n in range(outer):
        wsum[n] = dot(xt[outer_of((n + 1) % outer) * 2 + row], kv_grads, 1, 0)
    for n in range(outer):
        landed(wy_in.at[n], wy_recv.at[n])
        total = wsum[n] + wy_in[n].astype(jnp.float32)
        if n < outer - 1:
            w_out[n] = total.astype(jnp.bfloat16)
            send(w_out.at[n], w_in.at[n], w_recv.at[n], ctx_of(outer_of(n + 1), i_me), pair)
    for m in range(1, outer):
        landed(w_in.at[m - 1], w_recv.at[m - 1])
        total += w_in[m - 1].astype(jnp.float32)
    w_fin[pair] = total[:width]
    for e in range(1, pairs):
        send(w_fin.at[pair], w_fin.at[pair], fin_recv.at[e - 1], me, (pair + e) % pairs)
    for e in range(1, pairs):
        landed(w_fin.at[(pair + pairs - e) % pairs], fin_recv.at[e - 1])
    dw_ref[...] = w_fin[...].reshape(dw_ref.shape)
    for copy in pending:
        copy.wait_send()


def local(
    layer_input, queries, key_states, value_states, attn_output, out_grad, doc_ids, positions
):
    seqs, rows, model = layer_input.shape
    head = key_states.shape[2]
    ctx = lax.axis_size("ctx")
    pairs = lax.axis_size("dp")
    outer = ctx // INNER
    width = model // (ctx * pairs)
    padded = -(-width // LANES) * LANES
    slots = 2 * pairs
    flat_rows = seqs * rows
    flat = layer_input.reshape(flat_rows, model)
    if padded == width:
        x_parts = 2 * outer
    else:
        x_parts = 1
        flat = flat.reshape(flat_rows, 2 * outer, 2 * pairs, width).transpose(2, 1, 0, 3)
        flat = jnp.pad(flat, ((0, 0), (0, 0), (0, 0), (0, padded - width)))
    vmem = pl.BlockSpec(memory_space=pltpu.VMEM)
    both = 2 * head
    sends = HALVES * (4 * outer + 1) + 2 * GROUPS + 2 + GROUPS * outer
    sends += HALVES * (1 + 2 * (pairs - 1))
    sends += (slots - 1) * x_parts + outer + (outer - 1) + (pairs - 1)
    dma = pltpu.SemaphoreType.DMA
    f32, bf16 = jnp.float32, jnp.bfloat16
    step = rows // GROUPS
    query_width = queries.shape[2]
    query_grad, weight_grad = pl.pallas_call(
        functools.partial(kernel, (outer, pairs, width)),
        out_shape=(
            jax.ShapeDtypeStruct((flat_rows, query_width), bf16),
            jax.ShapeDtypeStruct((model // ctx, both), f32),
        ),
        in_specs=[pl.BlockSpec(memory_space=pl.ANY)] + [vmem] * 7,
        out_specs=(vmem, vmem),
        scratch_shapes=[
            pltpu.VMEM((ctx, rows, both), bf16),
            pltpu.VMEM((rows, both), bf16),
            pltpu.VMEM((rows, query_width), bf16),
            pltpu.VMEM((rows, query_width), bf16),
            pltpu.VMEM((8, LANES), f32),
            pltpu.VMEM((8, LANES), f32),
            pltpu.VMEM((8, LANES), f32),
            pltpu.VMEM((rows, query_width), bf16),
            pltpu.VMEM((rows, query_width), bf16),
            pltpu.VMEM((ctx, rows, LANES), f32),
            pltpu.VMEM((ctx * rows, LANES), f32),
            pltpu.VMEM((GROUPS, outer, 2, 2, step, both), f32),
            pltpu.VMEM((GROUPS, outer, 2, step, both), bf16),
            pltpu.VMEM((GROUPS, outer, 2, step, both), bf16),
            pltpu.VMEM((GROUPS, outer, 2, step, both), f32),
            pltpu.VMEM((GROUPS, outer - 1, 2, step, both), bf16),
            pltpu.VMEM((GROUPS, outer - 1, 2, step, both), bf16),
            pltpu.VMEM((2, rows, both), bf16),
            pltpu.VMEM((pairs, 2, seqs, rows, both), bf16),
            pltpu.VMEM((slots, 2 * outer, flat_rows, padded), bf16),
            pltpu.VMEM((2 * outer, padded, slots * flat_rows), bf16),
            pltpu.VMEM((outer, padded, both), f32),
            pltpu.VMEM((outer, padded, both), bf16),
            pltpu.VMEM((outer, padded, both), bf16),
            pltpu.VMEM((outer - 1, padded, both), bf16),
            pltpu.VMEM((outer - 1, padded, both), bf16),
            pltpu.VMEM((pairs, width, both), f32),
            dma((sends,)),
            dma((GROUPS, 2)),
            dma((2,)),
            dma((HALVES, ctx)),
            dma((GROUPS,)),
            dma((GROUPS, outer - 1)),
            dma((pairs, seqs, HALVES)),
            dma((slots - 1, x_parts)),
            dma((outer,)),
            dma((outer - 1,)),
            dma((pairs - 1,)),
            dma((x_parts,)),
        ],
        compiler_params=pltpu.CompilerParams(
            collective_id=0, has_side_effects=True, vmem_limit_bytes=60 * 1024 * 1024
        ),
    )(flat, queries, key_states, value_states, attn_output, out_grad, doc_ids, positions)
    return query_grad.reshape(queries.shape), weight_grad


def solution(mesh):
    in_specs = (
        P("dp", "ctx", None),
        P("dp", "ctx", None),
        P("dp", "ctx", None),
        P("dp", "ctx", None),
        P("dp", "ctx", None),
        P("dp", "ctx", None),
        P("dp", None),
        P("dp", None),
    )
    out_specs = (P("dp", "ctx", None), P("ctx", None))
    return jax.shard_map(local, mesh=mesh, in_specs=in_specs, out_specs=out_specs, check_vma=False)
```

```python
import functools
import math

import jax
import jax.numpy as jnp
from jax import lax
from jax.experimental import pallas as pl
from jax.experimental.pallas import tpu as pltpu
from jax.sharding import PartitionSpec as P

NEG_FILL = -1e30
INNER = 4
LANES = 128


GROUPS = 4
HALVES = GROUPS


def kernel(
    dims,
    x_ref,
    q_ref,
    k_ref,
    v_ref,
    a_ref,
    g_ref,
    doc_ref,
    pos_ref,
    dq_ref,
    dw_ref,
    kv,
    kv_swap,
    q_in,
    g_in,
    delta_own,
    delta_out,
    delta_in,
    dq_out,
    dq_in,
    kpos,
    dcol,
    acc,
    y_out,
    y_in,
    y_sum,
    z_out,
    z_in,
    z_sum,
    kvg,
    xg,
    xt,
    wsum,
    wy_out,
    wy_in,
    w_out,
    w_in,
    w_fin,
    send_sem,
    swap_recv,
    side_recv,
    ag_recv,
    y_recv,
    z_recv,
    kvg_recv,
    x_recv,
    wy_recv,
    w_recv,
    fin_recv,
    own_sem,
):
    outer, pairs, width = dims
    seqs, rows, head = k_ref.shape
    heads = q_ref.shape[2] // head
    step = rows // GROUPS
    scale = 1.0 / math.sqrt(head)
    x_parts = 2 * outer if x_ref.ndim == 2 else 1
    ctx_count = outer * INNER

    me = lax.axis_index("ctx")
    pair = lax.axis_index("dp")
    o_me, i_me = me // INNER, me % INNER
    col, row = i_me % 2, i_me // 2
    other = (col + 1) % 2

    def inner_of(k):
        return ((row + k // 2) % 2) * 2 + (col + k % 2) % 2

    def outer_of(m):
        return (o_me + m) % outer

    def ctx_of(o, i):
        return o * INNER + i

    side, across = ctx_of(o_me, inner_of(1)), ctx_of(o_me, inner_of(2))

    pending = []

    def copy_to(src, dst, recv_sem, ctx, dp, slot):
        return pltpu.make_async_remote_copy(
            src_ref=src,
            dst_ref=dst,
            send_sem=send_sem.at[slot],
            recv_sem=recv_sem,
            device_id={"ctx": ctx, "dp": dp},
            device_id_type=pl.DeviceIdType.MESH,
        )

    def send(src, dst, recv_sem, ctx, dp):
        copy = copy_to(src, dst, recv_sem, ctx, dp, len(pending))
        copy.start()
        pending.append(copy)

    def landed(dst, recv_sem):
        copy_to(dst, dst, recv_sem, side, pair, 0).wait_recv()

    slots = [(k, e) for k in range(2) for e in range(pairs)]

    barrier = pltpu.get_barrier_semaphore()
    greeted = [(ctx_of(outer_of(m), i_me), pair) for m in range(1, outer)]
    greeted += [(across, pair)]
    greeted += [(ctx_of(o_me, inner_of(k)), (pair + e) % pairs) for k, e in slots[1:]]
    for ctx, dp in greeted:
        pl.semaphore_signal(
            barrier,
            inc=1,
            device_id={"ctx": ctx, "dp": dp},
            device_id_type=pl.DeviceIdType.MESH,
        )

    def heads_of(block):
        return jnp.concatenate(
            [block[:, h * head : (h + 1) * head] for h in range(heads)], axis=0
        )

    def delta_rows(s, g):
        cut = slice(g * step, (g + 1) * step)
        product = heads_of(g_ref[s, cut, :].astype(jnp.float32)) * heads_of(
            a_ref[s, cut, :].astype(jnp.float32)
        )
        return jnp.sum(product.T, axis=0, keepdims=True)

    kv[me, :, 0:head] = k_ref[col]
    kv[me, :, head : 2 * head] = v_ref[col]
    kv_swap[:, 0:head] = k_ref[other]
    kv_swap[:, head : 2 * head] = v_ref[other]
    pl.semaphore_wait(barrier, len(greeted))

    def half(h):
        return pl.ds(h * (rows // HALVES), rows // HALVES)

    def block_send(src, h, ctx):
        send(kv.at[src, half(h)], kv.at[src, half(h)], ag_recv.at[h, src], ctx, pair)

    def block_landed(src, h):
        landed(kv.at[src, half(h)], ag_recv.at[h, src])

    for h in range(HALVES):
        send(kv_swap.at[half(h)], kv.at[me, half(h)], ag_recv.at[h, me], side, pair)
        for m in range(1, outer):
            block_send(me, h, ctx_of(outer_of(m), i_me))
        block_send(me, h, across)
    for g in range(GROUPS):
        cut = pl.ds(g * step, step)
        send(q_ref.at[other, cut], q_in.at[cut], swap_recv.at[g, 0], side, pair)
        send(g_ref.at[other, cut], g_in.at[cut], swap_recv.at[g, 1], side, pair)
    def x_source(o, i, d):
        if x_ref.ndim == 2:
            first = ((o * 2 + i) * pairs + d) * width
            return x_ref.at[:, pl.ds(pl.multiple_of(first, LANES), width)]
        return x_ref.at[i * pairs + d]

    def slot_of(k, e, column):
        return e * 2 + (column + k) % 2

    def x_target(n, o):
        return xg.at[n, o] if x_ref.ndim == 2 else xg.at[n]

    def slot_of(k, e, column):
        return e * 2 + (column + k) % 2

    def x_target(n, o):
        return xg.at[n, o] if x_ref.ndim == 2 else xg.at[n]

    own_copies = []
    for o in range(x_parts):
        own_copies.append(
            pltpu.make_async_copy(x_source(o, col, pair), x_target(slot_of(0, 0, col), o), own_sem.at[o])
        )
        own_copies[-1].start()

    def x_start(chosen):
        for n, (k, e) in enumerate(slots):
            if n and k == chosen:
                for o in range(x_parts):
                    send(
                        x_source(o, (col + k) % 2, (pair + e) % pairs),
                        x_target(slot_of(0, e, col), o),
                        x_recv.at[n - 1, o],
                        ctx_of(o_me, inner_of(k)),
                        (pair + e) % pairs,
                    )

    for h in range(HALVES):
        block_landed(side, h)
        for m in range(1, outer):
            block_send(side, h, ctx_of(outer_of(m), i_me))
        block_send(side, h, across)

    for g in range(GROUPS):
        delta_out[g : g + 1, :] = delta_rows(other, g)
    send(delta_out, delta_in, side_recv.at[0], side, pair)
    def forward(h):
        for m in range(1, outer):
            o = outer_of(outer - m)
            for src in (ctx_of(o, i_me), ctx_of(o, inner_of(1))):
                block_landed(src, h)
                block_send(src, h, across)

    forward(0)
    for g in range(GROUPS):
        delta_own[g : g + 1, :] = delta_rows(col, g)

    def columns_of(line):
        return jnp.broadcast_to(line, (LANES, LANES)).T

    total_rows = ctx_count * rows
    per = LANES // rows
    pos_line = pos_ref[pl.ds(col, 1), :].astype(jnp.float32)
    doc_line = doc_ref[pl.ds(col, 1), :].astype(jnp.float32)
    for b in range(total_rows // LANES):
        cut = slice(b * LANES, (b + 1) * LANES)
        kpos[b * per : (b + 1) * per] = columns_of(pos_line[:, cut]).reshape(per, rows, LANES)
        dcol[cut] = columns_of(doc_line[:, cut])

    forward(1)
    x_start(0)

    for h in range(2, HALVES):
        forward(h)
    own_rows = jnp.concatenate([kpos[me], kpos[side]], axis=0)
    sub = lax.broadcasted_iota(jnp.int32, own_rows.shape, 0)
    lane = lax.broadcasted_iota(jnp.int32, own_rows.shape, 1)
    row_pos = jnp.sum(jnp.where(sub == lane, own_rows, 0.0), axis=0, keepdims=True)
    place = lax.broadcasted_iota(jnp.int32, (total_rows, LANES), 0).astype(jnp.float32)
    doc_cols = dcol[...]
    row_doc = jnp.sum(jnp.where(place == row_pos, doc_cols, 0.0), axis=0, keepdims=True)
    row_first = jnp.sum(jnp.where(doc_cols < row_doc, 1.0, 0.0), axis=0, keepdims=True)
    first_rows = columns_of(row_first)
    pick = (sub == lane % step)[:step]

    def along(block):
        return jnp.sum(jnp.where(pick, block, 0.0), axis=0, keepdims=True)

    found = []
    for g in range(GROUPS):
        places = [slice(n * rows + g * step, n * rows + (g + 1) * step) for n in range(2)]
        found.append(
            tuple(
                jnp.concatenate([along(block[cut]) for cut in places], axis=1)
                for block in (own_rows, first_rows)
            )
        )

    def dot(a, b, ca, cb):
        return lax.dot_general(
            a, b, (((ca,), (cb,)), ((), ())), preferred_element_type=jnp.float32
        )

    def attend(g):
        pos, first = found[g]
        low, high = max(g - 1, 0) * step, (g + 1) * step
        span = high - low
        key_count = ctx_count * span
        cut = slice(g * step, (g + 1) * step)
        own_cut = pl.ds(pl.multiple_of(col * rows + g * step, step), step)
        key_block = kv[:, low:high, 0:head].reshape(key_count, head)
        value_block = kv[:, low:high, head : 2 * head].reshape(key_count, head)
        key_pos = kpos[:, low:high, :].reshape(key_count, LANES)
        key_pos = jnp.concatenate([key_pos, key_pos], axis=1)
        query_n = jnp.concatenate(
            [heads_of(q_ref[col, cut, :]), heads_of(q_in[cut, :])], axis=0
        )
        grad_n = jnp.concatenate(
            [heads_of(g_ref[col, cut, :]), heads_of(g_in[cut, :])], axis=0
        )
        delta = jnp.concatenate([delta_own[g : g + 1, :], delta_in[g : g + 1, :]], axis=1)
        live = (key_pos <= pos) & (key_pos >= first)
        scores = jnp.where(live, dot(key_block, query_n, 1, 1), NEG_FILL)
        drop = scores - jnp.max(scores, axis=0, keepdims=True)
        terms = jnp.exp2(drop * (scale * math.log2(math.e)))
        probs = terms * (1.0 / jnp.sum(terms, axis=0, keepdims=True))
        prob_grad = dot(value_block, grad_n, 1, 1)
        score_grad = (probs * (prob_grad - delta)).astype(jnp.bfloat16)
        value_grad = dot(probs.astype(jnp.bfloat16), grad_n, 1, 0)
        key_grad = dot(score_grad, query_n, 1, 0) * scale
        query_grad = (dot(score_grad, key_block, 0, 0) * scale).astype(jnp.bfloat16)
        for h in range(heads):
            cols = slice(h * head, (h + 1) * head)
            dq_ref[own_cut, cols] = query_grad[h * step : (h + 1) * step]
            dq_out[cut, cols] = query_grad[(heads + h) * step : (heads + h + 1) * step]
        for part, grad in ((0, key_grad), (1, value_grad)):
            grad = grad.reshape(outer, 2, 2, span, head)
            cols = slice(part * head, (part + 1) * head)
            if span > step:
                acc[g - 1, :, :, :, :, cols] += grad[:, :, :, :step]
            acc[g, :, :, :, :, cols] = grad[:, :, :, span - step :]

    def y_start(b):
        y_out[b] = acc[b, :, (row + 1) % 2].astype(jnp.bfloat16)
        send(y_out.at[b], y_in.at[b], y_recv.at[b], across, pair)

    def z_start(b):
        landed(y_in.at[b], y_recv.at[b])
        y_sum[b] = acc[b, :, row] + y_in[b].astype(jnp.float32)
        for m in range(1, outer):
            z_out[b, m - 1] = y_sum[b, outer_of(m)].astype(jnp.bfloat16)
            send(
                z_out.at[b, m - 1],
                z_in.at[b, m - 1],
                z_recv.at[b, m - 1],
                ctx_of(outer_of(m), i_me),
                pair,
            )

    def z_finish(b):
        total = y_sum[b, o_me]
        for m in range(1, outer):
            landed(z_in.at[b, m - 1], z_recv.at[b, m - 1])
            total += z_in[b, m - 1].astype(jnp.float32)
        z_sum[:, b * step : (b + 1) * step, :] = total.astype(jnp.bfloat16)

    def wait_half(h):
        for o in range(outer):
            for k in (2, 3):
                block_landed(ctx_of(outer_of(o), inner_of(k)), h)

    def kvg_at(e, s, h):
        return kvg.at[e, :, s, half(h)], kvg_recv.at[e, s, h]

    def pass_on(s, h):
        for e in range(1, pairs):
            dst, recv_sem = kvg_at(e, s, h)
            send(kvg_at(0, s, h)[0], dst, recv_sem, me, (pair + e) % pairs)

    def x_turn(chosen):
        for n, (k, e) in enumerate(slots):
            if k == chosen:
                for o in range(x_parts):
                    if n:
                        landed(x_target(slot_of(k, e, col), o), x_recv.at[n - 1, o])
                    else:
                        own_copies[o].wait()
                slot = slot_of(k, e, col)
                cut = pl.ds(pl.multiple_of(slot * (seqs * rows), seqs * rows), seqs * rows)
                for o in range(2 * outer):
                    xt[o, :, cut] = xg[slot, o].T

    wait_half(0)
    landed(delta_in, side_recv.at[0])
    for g in range(GROUPS):
        cut = pl.ds(g * step, step)
        landed(q_in.at[cut], swap_recv.at[g, 0])
        landed(g_in.at[cut], swap_recv.at[g, 1])
        if g > 0:
            wait_half(g)
        if g == 0:
            x_start(1)
        attend(g)
        if g >= 1:
            y_start(g - 1)
        if g >= 2:
            z_start(g - 2)
    y_start(GROUPS - 1)
    z_start(GROUPS - 2)
    z_start(GROUPS - 1)
    x_turn(0)
    for h in range(HALVES):
        for b in range(h * GROUPS // HALVES, (h + 1) * GROUPS // HALVES):
            z_finish(b)
        dst, recv_sem = kvg_at(0, col, h)
        send(z_sum.at[:, half(h)], dst, recv_sem, side, pair)
        kvg[0, :, col, half(h)] = z_sum[:, half(h)]
        pass_on(col, h)
    send(dq_out, dq_in, side_recv.at[1], side, pair)
    x_turn(1)
    for h in range(HALVES):
        landed(*kvg_at(0, other, h))
        pass_on(other, h)
    landed(dq_in, side_recv.at[1])
    dq_ref[pl.ds(pl.multiple_of(other * rows, rows), rows), :] = dq_in[...]
    for e in range(1, pairs):
        for s in range(seqs):
            for h in range(HALVES):
                landed(*kvg_at(e, s, h))

    depth = len(slots) * seqs * rows
    kv_grads = kvg[...].reshape(depth, 2 * head)
    for n in range(outer):
        o = outer_of((n + 1) % outer)
        wy_out[n] = dot(xt[o * 2 + (row + 1) % 2], kv_grads, 1, 0).astype(jnp.bfloat16)
        send(wy_out.at[n], wy_in.at[n], wy_recv.at[n], across, pair)
    for n in range(outer):
        wsum[n] = dot(xt[outer_of((n + 1) % outer) * 2 + row], kv_grads, 1, 0)
    for n in range(outer):
        landed(wy_in.at[n], wy_recv.at[n])
        total = wsum[n] + wy_in[n].astype(jnp.float32)
        if n < outer - 1:
            w_out[n] = total.astype(jnp.bfloat16)
            send(w_out.at[n], w_in.at[n], w_recv.at[n], ctx_of(outer_of(n + 1), i_me), pair)
    for m in range(1, outer):
        landed(w_in.at[m - 1], w_recv.at[m - 1])
        total += w_in[m - 1].astype(jnp.float32)
    w_fin[pair] = total[:width]
    for e in range(1, pairs):
        send(w_fin.at[pair], w_fin.at[pair], fin_recv.at[e - 1], me, (pair + e) % pairs)
    for e in range(1, pairs):
        landed(w_fin.at[(pair + pairs - e) % pairs], fin_recv.at[e - 1])
    dw_ref[...] = w_fin[...].reshape(dw_ref.shape)
    for copy in pending:
        copy.wait_send()


def local(
    layer_input, queries, key_states, value_states, attn_output, out_grad, doc_ids, positions
):
    seqs, rows, model = layer_input.shape
    head = key_states.shape[2]
    ctx = lax.axis_size("ctx")
    pairs = lax.axis_size("dp")
    outer = ctx // INNER
    width = model // (ctx * pairs)
    padded = -(-width // LANES) * LANES
    slots = 2 * pairs
    flat_rows = seqs * rows
    flat = layer_input.reshape(flat_rows, model)
    if padded == width:
        x_parts = 2 * outer
    else:
        x_parts = 1
        flat = flat.reshape(flat_rows, 2 * outer, 2 * pairs, width).transpose(2, 1, 0, 3)
        flat = jnp.pad(flat, ((0, 0), (0, 0), (0, 0), (0, padded - width)))
    vmem = pl.BlockSpec(memory_space=pltpu.VMEM)
    both = 2 * head
    sends = HALVES * (4 * outer + 1) + 2 * GROUPS + 2 + GROUPS * outer
    sends += HALVES * (1 + 2 * (pairs - 1))
    sends += (slots - 1) * x_parts + outer + (outer - 1) + (pairs - 1)
    dma = pltpu.SemaphoreType.DMA
    f32, bf16 = jnp.float32, jnp.bfloat16
    step = rows // GROUPS
    query_width = queries.shape[2]
    query_grad, weight_grad = pl.pallas_call(
        functools.partial(kernel, (outer, pairs, width)),
        out_shape=(
            jax.ShapeDtypeStruct((flat_rows, query_width), bf16),
            jax.ShapeDtypeStruct((model // ctx, both), f32),
        ),
        in_specs=[pl.BlockSpec(memory_space=pl.ANY)] + [vmem] * 7,
        out_specs=(vmem, vmem),
        scratch_shapes=[
            pltpu.VMEM((ctx, rows, both), bf16),
            pltpu.VMEM((rows, both), bf16),
            pltpu.VMEM((rows, query_width), bf16),
            pltpu.VMEM((rows, query_width), bf16),
            pltpu.VMEM((8, LANES), f32),
            pltpu.VMEM((8, LANES), f32),
            pltpu.VMEM((8, LANES), f32),
            pltpu.VMEM((rows, query_width), bf16),
            pltpu.VMEM((rows, query_width), bf16),
            pltpu.VMEM((ctx, rows, LANES), f32),
            pltpu.VMEM((ctx * rows, LANES), f32),
            pltpu.VMEM((GROUPS, outer, 2, 2, step, both), f32),
            pltpu.VMEM((GROUPS, outer, 2, step, both), bf16),
            pltpu.VMEM((GROUPS, outer, 2, step, both), bf16),
            pltpu.VMEM((GROUPS, outer, 2, step, both), f32),
            pltpu.VMEM((GROUPS, outer - 1, 2, step, both), bf16),
            pltpu.VMEM((GROUPS, outer - 1, 2, step, both), bf16),
            pltpu.VMEM((2, rows, both), bf16),
            pltpu.VMEM((pairs, 2, seqs, rows, both), bf16),
            pltpu.VMEM((slots, 2 * outer, flat_rows, padded), bf16),
            pltpu.VMEM((2 * outer, padded, slots * flat_rows), bf16),
            pltpu.VMEM((outer, padded, both), f32),
            pltpu.VMEM((outer, padded, both), bf16),
            pltpu.VMEM((outer, padded, both), bf16),
            pltpu.VMEM((outer - 1, padded, both), bf16),
            pltpu.VMEM((outer - 1, padded, both), bf16),
            pltpu.VMEM((pairs, width, both), f32),
            dma((sends,)),
            dma((GROUPS, 2)),
            dma((2,)),
            dma((HALVES, ctx)),
            dma((GROUPS,)),
            dma((GROUPS, outer - 1)),
            dma((pairs, seqs, HALVES)),
            dma((slots - 1, x_parts)),
            dma((outer,)),
            dma((outer - 1,)),
            dma((pairs - 1,)),
            dma((x_parts,)),
        ],
        compiler_params=pltpu.CompilerParams(
            collective_id=0, has_side_effects=True, vmem_limit_bytes=60 * 1024 * 1024
        ),
    )(flat, queries, key_states, value_states, attn_output, out_grad, doc_ids, positions)
    return query_grad.reshape(queries.shape), weight_grad


def solution(mesh):
    in_specs = (
        P("dp", "ctx", None),
        P("dp", "ctx", None),
        P("dp", "ctx", None),
        P("dp", "ctx", None),
        P("dp", "ctx", None),
        P("dp", "ctx", None),
        P("dp", None),
        P("dp", None),
    )
    out_specs = (P("dp", "ctx", None), P("ctx", None))
    return jax.shard_map(local, mesh=mesh, in_specs=in_specs, out_specs=out_specs, check_vma=False)
```
